32 devices in a mesh: dp: 4 (over y, x), pipe: 4 (over z), tensor: 2 (over core).
Axes of the slice: x: 2, y: 2, z: 4, core: 2. Of those that a mesh axis runs over, the one named last changes fastest.
Arguments:
- enc_out: bfloat16 [512, 4096], P('dp', 'tensor'), may hold values from -1.25 to 1.25
- mlp_input: bfloat16 [512, 4096], P('dp', 'tensor'), may hold values from -170 to 170
- grad_kv: bfloat16 [512, 2, 4, 512], P('dp', None, 'pipe', 'tensor'), may hold values from -1.5 to 1.5
- kv_weight: bfloat16 [4096, 2, 4, 512], P('dp', None, 'pipe', 'tensor'), may hold values from -0.09375 to 0.09375
- gate_weight: bfloat16 [4096, 1024], P('dp', ('pipe', 'tensor')), may hold values from -0.09375 to 0.09375
- up_weight: bfloat16 [4096, 1024], P('dp', ('pipe', 'tensor')), may hold values from -0.09375 to 0.09375
- down_weight: bfloat16 [1024, 4096], P(('pipe', 'tensor'), 'dp'), may hold values from -0.1875 to 0.1875
- norm_gain: bfloat16 [4096], replicated, may hold values from 0.099609375 to 1.8984375
Outputs:
- input_grad: bfloat16 [512, 4096], P('dp')
- kv_grad: bfloat16 [4096, 2, 4, 512], P('dp', None, 'pipe', 'tensor')
The draws below stay inside these ranges and needn't reach their ends.
All inputs are finite; a program needn't handle non-finite values.
Results may differ from the reference program's by a relative error of at most 0.009.
Values may be sent and summed in bfloat16 or wider, within the bound.
No kernel may reach another device: no remote copies, remote signals or barrier semaphores. Data moves between devices by JAX's collectives and lax.ppermute only.
A program may use at most 64 MiB of HBM per device.

```python
import math
import jax
import jax.numpy as jnp
from jax import lax

D = 4096
TOK = 128
FF = 1024
HEAD_COLS = 512
LAYERS = 4
TOKENS = 512
N_DP = 4


def draw_mlp_input(key, part):
    key_rows, key_cols, key_base = jax.random.split(key, 3)
    row_scales = jnp.exp(jax.random.uniform(key_rows, (TOKENS, 1), jnp.float32, 0.0, jnp.log(10.0)))
    col_scales = jnp.exp(jax.random.uniform(key_cols, (1, D), jnp.float32, 0.0, jnp.log(10.0)))
    base = jax.random.normal(key_base, (TOKENS, D), jnp.float32)
    base = jnp.clip(base, -5.0, 5.0)
    return (base * row_scales * col_scales / 3.0).astype(jnp.bfloat16)


def level_of(key, dims, cuts, least, top_value):
    def one(axis_at, shards_of):
        steps = jax.random.uniform(jax.random.fold_in(jax.random.fold_in(key, 6), axis_at), (shards_of,), jnp.float32, least / len(cuts), top_value / len(cuts))
        return jnp.repeat(jnp.exp(steps), dims[axis_at] // shards_of).reshape((-1,) + (1,) * (len(dims) - axis_at - 1))

    gain = one(*cuts[0])
    for cut in cuts[1:]:
        gain = gain * one(*cut)
    return gain


def normal_values(rng, dims, deviation, most, shards=(), dtype=jnp.bfloat16):
    values = jax.random.normal(rng, dims, jnp.float32) * deviation
    if len(shards) > 0:
        values = level_of(rng, dims, shards, -0.22, 0.18) * values
    return jnp.clip(values, min=-most, max=most).astype(dtype)


def setup_inputs(seed: int = 0) -> dict:
    streams_of = jax.random.split(jax.random.key(seed), 9)
    enc_out = normal_values(streams_of[0], (TOKENS, D), 0.2, 1.25, ((0, 4), (1, 2)))
    mlp_input = draw_mlp_input(jax.random.fold_in(streams_of[8], 71), 0)
    grad_kv = normal_values(streams_of[2], (TOKENS, 2, LAYERS, HEAD_COLS), 0.25, 1.5, ((0, 4), (2, 4), (3, 2)))
    kv_weight = normal_values(streams_of[3], (D, 2, LAYERS, HEAD_COLS), D ** -0.5, 0.09375, ((0, 4), (2, 4), (3, 2)))
    gate_weight = normal_values(streams_of[4], (D, FF), D ** -0.5, 0.09375, ((0, 4), (1, 8)))
    up_weight = normal_values(streams_of[5], (D, FF), D ** -0.5, 0.09375, ((0, 4), (1, 8)))
    down_weight = normal_values(streams_of[6], (FF, D), FF ** -0.5, 0.1875, ((0, 8), (1, 4)))
    norm_gain = jnp.clip(1.0 + 0.18 * jax.random.normal(streams_of[7], (D,), jnp.float32), 0.099609375, 1.8984375).astype(jnp.bfloat16)
    return dict(enc_out=enc_out, mlp_input=mlp_input, grad_kv=grad_kv, kv_weight=kv_weight, gate_weight=gate_weight, up_weight=up_weight, down_weight=down_weight, norm_gain=norm_gain)


def gelu_parts(preact):
    factor = math.sqrt(2.0 / math.pi)
    tangent = jnp.tanh(factor * (preact + 0.044715 * preact * preact * preact))
    gelu_value = 0.5 * preact * (1.0 + tangent)
    gelu_slope = 0.5 * (1.0 + tangent) + 0.5 * preact * (1.0 - tangent * tangent) * factor * (1.0 + 3.0 * 0.044715 * preact * preact)
    return (gelu_value, gelu_slope)

def reference(enc_out, mlp_input, grad_kv, kv_weight, gate_weight, up_weight, down_weight, norm_gain):
    upstream = jnp.zeros((TOKENS, D), jnp.float32)
    layer_grads = []
    for layer_idx in range(LAYERS):
        grad_here = grad_kv[:, :, layer_idx, :].astype(jnp.float32)
        weight_here = kv_weight[:, :, layer_idx, :].astype(jnp.float32)
        upstream = upstream + jnp.einsum('tsc,dsc->td', grad_here, weight_here)
        summed = jnp.zeros((D, 2, HEAD_COLS), jnp.float32)
        for replica in range(N_DP):
            rows_enc = enc_out[replica * TOK:(replica + 1) * TOK].astype(jnp.float32)
            rows_grad = grad_here[replica * TOK:(replica + 1) * TOK]
            replica_term = jnp.einsum('td,tsc->dsc', rows_enc, rows_grad).astype(jnp.bfloat16)
            replica_term = lax.optimization_barrier(replica_term)
            summed = summed + replica_term.astype(jnp.float32)
        layer_grads.append(summed.astype(jnp.bfloat16))
    kv_grad = jnp.stack(layer_grads, axis=2)
    upstream_half = upstream.astype(jnp.bfloat16)
    values_in = mlp_input.astype(jnp.float32)
    row_scale = lax.rsqrt(lax.optimization_barrier(jnp.mean(values_in * values_in, axis=1, keepdims=True)) + 1e-06)
    gain_row = norm_gain.astype(jnp.float32)
    normed = (values_in * row_scale * gain_row).astype(jnp.bfloat16)
    gate_pre = jnp.dot(normed, gate_weight, preferred_element_type=jnp.float32)
    up_pre = jnp.dot(normed, up_weight, preferred_element_type=jnp.float32)
    hidden_grad = jnp.dot(upstream_half, down_weight.T, preferred_element_type=jnp.float32)
    gelu_value, gelu_slope = gelu_parts(gate_pre)
    gate_grad = (hidden_grad * up_pre * gelu_slope).astype(jnp.bfloat16)
    up_grad = (hidden_grad * gelu_value).astype(jnp.bfloat16)
    normed_grad = jnp.dot(gate_grad, gate_weight.T, preferred_element_type=jnp.float32) + jnp.dot(up_grad, up_weight.T, preferred_element_type=jnp.float32)
    scaled_grad = gain_row * normed_grad
    input_grad = upstream + row_scale * scaled_grad - values_in * (row_scale * row_scale * row_scale) * lax.optimization_barrier(jnp.mean(values_in * scaled_grad, axis=1, keepdims=True))
    return (input_grad.astype(jnp.bfloat16), kv_grad)
```

```python
import math

import jax
import jax.numpy as jnp
from jax import lax
from jax.sharding import PartitionSpec as P

DP, PIPE, TENSOR = "dp", "pipe", "tensor"
BF16, F32 = jnp.bfloat16, jnp.float32


def gelu_parts(preact):
    factor = math.sqrt(2.0 / math.pi)
    tangent = jnp.tanh(factor * (preact + 0.044715 * preact * preact * preact))
    gelu_value = 0.5 * preact * (1.0 + tangent)
    gelu_slope = 0.5 * (1.0 + tangent) + 0.5 * preact * (1.0 - tangent * tangent) * factor * (
        1.0 + 3.0 * 0.044715 * preact * preact
    )
    return (gelu_value, gelu_slope)


def send(value, axis, step):
    if step == 0:
        return value
    size = lax.axis_size(axis)
    return lax.ppermute(value, axis, [(src, src ^ step) for src in range(size)])


def gather(value, axis):
    return [send(value, axis, step) for step in range(lax.axis_size(axis))]


def natural(parts, axis, dim):
    mine = lax.axis_index(axis)
    width = parts[0].shape[dim]
    shape = list(parts[0].shape)
    shape[dim] = width * len(parts)
    out = jnp.zeros(shape, parts[0].dtype)
    for step, part in enumerate(parts):
        out = lax.dynamic_update_slice_in_dim(out, part, (mine ^ step) * width, dim)
    return out


def block(value, axis, step, dim):
    width = value.shape[dim] // lax.axis_size(axis)
    start = (lax.axis_index(axis) ^ step) * width
    return lax.dynamic_slice_in_dim(value, start, width, dim)


def total(blocks, axis):
    out = blocks[0].astype(F32)
    for step in range(1, len(blocks)):
        out = out + send(blocks[step].astype(BF16), axis, step).astype(F32)
    return out


def dot_nt(left, right):
    return lax.dot_general(left, right, (((1,), (1,)), ((), ())), preferred_element_type=F32)


def on_device(
    enc_out, mlp_input, grad_kv, kv_weight, gate_weight, up_weight, down_weight, norm_gain
):
    n_dp, n_pipe, n_ten = (lax.axis_size(a) for a in (DP, PIPE, TENSOR))
    tok = grad_kv.shape[0]
    width = norm_gain.shape[0]
    cols = kv_weight.shape[0]
    units = gate_weight.shape[1]
    share = cols // (n_pipe * n_ten)

    grads = jnp.concatenate(gather(grad_kv.reshape(tok, -1), DP), axis=0)

    section = kv_weight.reshape(cols, -1)
    partial = dot_nt(grads, section)
    partial = total([block(partial, TENSOR, k, 1) for k in range(n_ten)], TENSOR)
    partial = total([block(partial, PIPE, k, 1) for k in range(n_pipe)], PIPE)
    partial = partial.astype(BF16).reshape(n_dp, tok, share)
    upstream = jnp.concatenate([send(partial[k], DP, k) for k in range(n_dp)], axis=1)

    down = jnp.concatenate([send(block(down_weight, TENSOR, k, 1), TENSOR, k) for k in range(n_ten)], axis=0)
    down = jnp.concatenate([send(block(down, PIPE, k, 1), PIPE, k) for k in range(n_pipe)], axis=0)
    down = jnp.concatenate(gather(down, DP), axis=1)
    hidden = dot_nt(upstream, down).reshape(tok, n_pipe, n_ten, units)
    hidden = total([hidden[:, :, k] for k in range(n_ten)], TENSOR)
    hidden_grad = total([hidden[:, k] for k in range(n_pipe)], PIPE)

    both = jnp.concatenate([gate_weight, up_weight], axis=1)
    both = jnp.concatenate(gather(both, DP), axis=0)
    resid = natural(gather(mlp_input, TENSOR), TENSOR, 1)
    resid = jnp.concatenate([block(resid, DP, k, 1) for k in range(n_dp)], axis=1)
    gain_row = jnp.concatenate([block(norm_gain, DP, k, 0) for k in range(n_dp)], axis=0).astype(F32)
    values_in = resid.astype(F32)
    row_scale = lax.rsqrt(jnp.mean(values_in * values_in, axis=1, keepdims=True) + 1e-06)
    normed = (values_in * row_scale * gain_row).astype(BF16)
    pre = jnp.dot(normed, both, preferred_element_type=F32)
    gate_pre, up_pre = pre[:, :units], pre[:, units:]

    gelu_value, gelu_slope = gelu_parts(gate_pre)
    gate_grad = hidden_grad * up_pre * gelu_slope
    up_grad = hidden_grad * gelu_value
    dotted = jnp.sum(gate_grad * gate_pre + up_grad * up_pre, axis=1, keepdims=True)
    grads_both = jnp.concatenate([gate_grad, up_grad], axis=1).astype(BF16)
    normed_part = dot_nt(grads_both, both)
    part = row_scale * gain_row * normed_part - values_in * (row_scale * row_scale * (dotted / width))

    part = part.reshape(tok, n_dp, cols)
    part = total([block(part, TENSOR, k, 2) for k in range(n_ten)], TENSOR)
    part = total([block(part, PIPE, k, 2) for k in range(n_pipe)], PIPE)
    part = (part + upstream.reshape(tok, n_dp, share).astype(F32)).astype(BF16)
    whole = natural(gather(part, PIPE), PIPE, 2)
    whole = natural(gather(whole, TENSOR), TENSOR, 2)
    input_grad = natural([whole[:, k] for k in range(n_dp)], DP, 1)

    encoded = natural(gather(enc_out, TENSOR), TENSOR, 1)
    mine = [send(block(block(encoded, DP, k, 1), TENSOR, 0, 1), DP, k) for k in range(n_dp)]
    mine = jnp.concatenate(mine, axis=0)
    mine = natural(gather(mine, TENSOR), TENSOR, 1)
    kv_grad = lax.dot_general(
        mine, grads, (((0,), (0,)), ((), ())), preferred_element_type=F32
    ).astype(BF16)
    return (input_grad, kv_grad.reshape(kv_weight.shape))


def solution(mesh):
    placed = (
        P(DP, TENSOR),
        P(DP, TENSOR),
        P(DP, None, PIPE, TENSOR),
        P(DP, None, PIPE, TENSOR),
        P(DP, (PIPE, TENSOR)),
        P(DP, (PIPE, TENSOR)),
        P((PIPE, TENSOR), DP),
        P(),
    )
    return jax.shard_map(
        on_device,
        mesh=mesh,
        in_specs=placed,
        out_specs=(P(DP, None), P(DP, None, PIPE, TENSOR)),
        check_vma=False,
    )
```

```python
import math

import jax
import jax.numpy as jnp
from jax import lax
from jax.experimental import pallas as pl
from jax.experimental.pallas import tpu as pltpu
from jax.sharding import PartitionSpec as P

DP, PIPE, TENSOR = "dp", "pipe", "tensor"
BF16, F32 = jnp.bfloat16, jnp.float32


def gelu_parts(preact):
    factor = math.sqrt(2.0 / math.pi)
    tangent = jnp.tanh(factor * (preact + 0.044715 * preact * preact * preact))
    gelu_value = 0.5 * preact * (1.0 + tangent)
    gelu_slope = 0.5 * (1.0 + tangent) + 0.5 * preact * (1.0 - tangent * tangent) * factor * (
        1.0 + 3.0 * 0.044715 * preact * preact
    )
    return (gelu_value, gelu_slope)


def send(value, axis, step):
    if step == 0:
        return value
    size = lax.axis_size(axis)
    return lax.ppermute(value, axis, [(src, src ^ step) for src in range(size)])


def gather(value, axis):
    return [send(value, axis, step) for step in range(lax.axis_size(axis))]


def relayed(value, axis):
    far, near = send(value, axis, 2), send(value, axis, 1)
    return [value, near, far, send(far, axis, 1)]


def natural(parts, axis, dim):
    mine = lax.axis_index(axis)
    width = parts[0].shape[dim]
    shape = list(parts[0].shape)
    shape[dim] = width * len(parts)
    out = jnp.zeros(shape, parts[0].dtype)
    for step, part in enumerate(parts):
        out = lax.dynamic_update_slice_in_dim(out, part, (mine ^ step) * width, dim)
    return out


def block(value, axis, step, dim):
    width = value.shape[dim] // lax.axis_size(axis)
    start = (lax.axis_index(axis) ^ step) * width
    return lax.dynamic_slice_in_dim(value, start, width, dim)


def total(blocks, axis):
    out = blocks[0].astype(F32)
    for step in range(1, len(blocks)):
        out = out + send(blocks[step].astype(BF16), axis, step).astype(F32)
    return out


def dot_nt(left, right):
    return lax.dot_general(left, right, (((1,), (1,)), ((), ())), preferred_element_type=F32)


def on_device_any(
    enc_out, mlp_input, grad_kv, kv_weight, gate_weight, up_weight, down_weight, norm_gain
):
    n_dp, n_pipe, n_ten = (lax.axis_size(a) for a in (DP, PIPE, TENSOR))
    tok = grad_kv.shape[0]
    width = norm_gain.shape[0]
    cols = kv_weight.shape[0]
    units = gate_weight.shape[1]
    share = cols // (n_pipe * n_ten)

    grads = jnp.concatenate(gather(grad_kv.reshape(tok, -1), DP), axis=0)

    section = kv_weight.reshape(cols, -1)
    partial = dot_nt(grads, section)
    partial = total([block(partial, TENSOR, k, 1) for k in range(n_ten)], TENSOR)
    partial = total([block(partial, PIPE, k, 1) for k in range(n_pipe)], PIPE)
    partial = partial.astype(BF16).reshape(n_dp, tok, share)
    upstream = jnp.concatenate([send(partial[k], DP, k) for k in range(n_dp)], axis=1)

    down = jnp.concatenate([send(block(down_weight, TENSOR, k, 1), TENSOR, k) for k in range(n_ten)], axis=0)
    down = jnp.concatenate([send(block(down, PIPE, k, 1), PIPE, k) for k in range(n_pipe)], axis=0)
    down = jnp.concatenate(gather(down, DP), axis=1)
    hidden = dot_nt(upstream, down).reshape(tok, n_pipe, n_ten, units)
    hidden = total([hidden[:, :, k] for k in range(n_ten)], TENSOR)
    hidden_grad = total([hidden[:, k] for k in range(n_pipe)], PIPE)

    both = jnp.concatenate([gate_weight, up_weight], axis=1)
    both = jnp.concatenate(gather(both, DP), axis=0)
    resid = natural(gather(mlp_input, TENSOR), TENSOR, 1)
    resid = jnp.concatenate([block(resid, DP, k, 1) for k in range(n_dp)], axis=1)
    gain_row = jnp.concatenate([block(norm_gain, DP, k, 0) for k in range(n_dp)], axis=0).astype(F32)
    values_in = resid.astype(F32)
    row_scale = lax.rsqrt(jnp.mean(values_in * values_in, axis=1, keepdims=True) + 1e-06)
    normed = (values_in * row_scale * gain_row).astype(BF16)
    pre = jnp.dot(normed, both, preferred_element_type=F32)
    gate_pre, up_pre = pre[:, :units], pre[:, units:]

    gelu_value, gelu_slope = gelu_parts(gate_pre)
    gate_grad = hidden_grad * up_pre * gelu_slope
    up_grad = hidden_grad * gelu_value
    dotted = jnp.sum(gate_grad * gate_pre + up_grad * up_pre, axis=1, keepdims=True)
    grads_both = jnp.concatenate([gate_grad, up_grad], axis=1).astype(BF16)
    normed_part = dot_nt(grads_both, both)
    part = row_scale * gain_row * normed_part - values_in * (row_scale * row_scale * (dotted / width))

    part = part.reshape(tok, n_dp, cols)
    part = total([block(part, TENSOR, k, 2) for k in range(n_ten)], TENSOR)
    part = total([block(part, PIPE, k, 2) for k in range(n_pipe)], PIPE)
    part = (part + upstream.reshape(tok, n_dp, share).astype(F32)).astype(BF16)
    whole = natural(gather(part, PIPE), PIPE, 2)
    whole = natural(gather(whole, TENSOR), TENSOR, 2)
    input_grad = natural([whole[:, k] for k in range(n_dp)], DP, 1)

    encoded = natural(gather(enc_out, TENSOR), TENSOR, 1)
    mine = [send(block(block(encoded, DP, k, 1), TENSOR, 0, 1), DP, k) for k in range(n_dp)]
    mine = jnp.concatenate(mine, axis=0)
    mine = natural(gather(mine, TENSOR), TENSOR, 1)
    kv_grad = lax.dot_general(
        mine, grads, (((0,), (0,)), ((), ())), preferred_element_type=F32
    ).astype(BF16)
    return (input_grad, kv_grad.reshape(kv_weight.shape))


def aligned(start, lanes):
    return pl.ds(pl.multiple_of(start, lanes), lanes)


def call(body, name, out, operands, scratch=(), flops=0):
    specs = [pl.BlockSpec(memory_space=pltpu.SMEM)]
    specs += [pl.BlockSpec(memory_space=pltpu.VMEM)] * (len(operands) - 1)
    moved = sum(a.size * a.dtype.itemsize for a in (*operands, *out))
    return pl.pallas_call(
        body,
        name=name,
        out_shape=out,
        in_specs=specs,
        out_specs=[pl.BlockSpec(memory_space=pltpu.VMEM)] * len(out),
        scratch_shapes=list(scratch),
        compiler_params=pltpu.CompilerParams(vmem_limit_bytes=40 * 1024 * 1024),
        cost_estimate=pl.CostEstimate(flops=flops, bytes_accessed=moved, transcendentals=0),
    )(*operands)


def shaped(shape, dtype):
    return jax.ShapeDtypeStruct(shape, dtype)


def pack_kernel(where, gate, up, out):
    cols = gate.shape[0]
    out[:cols, :] = gate[...]
    out[cols:, :] = up[...]


def upstream_kernel(n_dp, where, *refs):
    pieces, (section, out, grads) = refs[:n_dp], refs[n_dp:]
    tok = pieces[0].shape[0]
    for k, piece in enumerate(pieces):
        grads[k * tok : (k + 1) * tok, :] = piece[...]
    out[...] = dot_nt(grads[...], section[...]).astype(out.dtype)


def hidden_kernel(n_dp, n_pipe, n_ten, where, mine, other, *refs):
    downs, (own_hidden, own_upstream), outs = refs[:n_pipe], refs[n_pipe : n_pipe + 2], refs[n_pipe + 2 : -2]
    upstream, down = refs[-2:]
    upstream[...] = (mine[...].astype(F32) + other[...].astype(F32)).astype(BF16)
    units = downs[0].shape[0]
    for k, part in enumerate(downs):
        down[k * units : (k + 1) * units, :] = part[...]
    result = dot_nt(upstream[...], down[...])
    tok, width = own_hidden.shape
    half = upstream.shape[1] // n_ten
    spot = aligned(where[2] * half, half)
    own_hidden[...] = result[:tok, :]
    own_upstream[...] = upstream[:tok, spot]
    for k, out in enumerate(outs, 1):
        out[:, :width] = result[k * tok : (k + 1) * tok, :].astype(BF16)
        out[:, width:] = upstream[k * tok : (k + 1) * tok, spot]


def forward_kernel(n_dp, where, *refs):
    packs, (x_mine, x_other, gain, resid, scale, pre, normed) = refs[:n_dp], refs[n_dp:]
    ten = where[2]
    half = x_mine.shape[1]
    resid[:, aligned(ten * half, half)] = x_mine[...]
    resid[:, aligned((ten ^ 1) * half, half)] = x_other[...]
    values_in = resid[...].astype(F32)
    row_scale = lax.rsqrt(jnp.mean(values_in * values_in, axis=1, keepdims=True) + 1e-06)
    scale[...] = jnp.broadcast_to(row_scale, scale.shape)
    normed[...] = (values_in * row_scale * gain[...].astype(F32)).astype(BF16)
    cols = resid.shape[1] // n_dp
    result = jnp.zeros(pre.shape, F32)
    for k, pack in enumerate(packs):
        left = normed[:, aligned((where[0] ^ k) * cols, cols)]
        right = jnp.concatenate([pack[:cols, :], pack[cols:, :]], axis=1)
        result += jnp.dot(left, right, preferred_element_type=F32)
    pre[...] = result


def backward_kernel(n_dp, n_pipe, n_ten, where, *refs):
    terms, ups, packs = refs[:n_pipe], refs[n_pipe : n_pipe + n_dp], refs[n_pipe + n_dp : n_pipe + 2 * n_dp]
    pre, scale, resid, gain, other, mine = refs[n_pipe + 2 * n_dp :]
    pipe, ten = where[1], where[2]
    hidden_grad = terms[0][...]
    for term in terms[1:]:
        hidden_grad = hidden_grad + term[...].astype(F32)
    units = hidden_grad.shape[1]
    gate_pre, up_pre = pre[:, :units], pre[:, units:]
    gelu_value, gelu_slope = gelu_parts(gate_pre)
    gate_grad = hidden_grad * up_pre * gelu_slope
    up_grad = hidden_grad * gelu_value
    dotted = jnp.sum(gate_grad * gate_pre + up_grad * up_pre, axis=1, keepdims=True)
    grads = jnp.concatenate([gate_grad, up_grad], axis=1).astype(BF16)
    row_scale = scale[:, :1]
    width = resid.shape[1]
    pull = row_scale * row_scale * (dotted / width)
    cols = width // n_dp
    half = cols // n_ten
    share = half // n_pipe
    for step, out in ((1, other), (0, mine)):
        start = (ten ^ step) * half
        for k, pack in enumerate(packs):
            i = where[0] ^ k
            spot = aligned(i * cols + start, half)
            rows = [pack[aligned(start, half), :], pack[aligned(cols + start, half), :]]
            part = dot_nt(grads, jnp.concatenate(rows, axis=1))
            part = row_scale * (gain[:, spot].astype(F32) * part) - resid[:, spot].astype(F32) * pull
            if step == 0:
                part = part + ups[k][:, ups[k].shape[1] - half :].astype(F32)
            part = part.astype(out.dtype)
            for j in range(n_pipe):
                out[pipe ^ j, :, aligned(i * share, share)] = part[:, j * share : (j + 1) * share]


def assemble_kernel(n_dp, n_pipe, n_ten, where, *refs):
    parts, out = refs[:-1], refs[-1]
    pipe, ten = where[1], where[2]
    share = parts[0].shape[1] // n_dp
    for core in range(n_ten):
        for k in range(n_pipe):
            part = parts[core * n_pipe + k]
            for i in range(n_dp):
                start = ((i * n_ten + (ten ^ core)) * n_pipe + (pipe ^ k)) * share
                out[:, aligned(start, share)] = part[:, i * share : (i + 1) * share]


def encoded_kernel(n_dp, n_ten, where, mine, other, own, near, far):
    dp, ten = where[0], where[2]
    tok, half = own.shape
    held = n_dp // n_ten
    for k, out in ((0, own), (1, near.at[:tok]), (3, near.at[tok:]), (2, far)):
        i = dp ^ k
        spot = aligned((lax.rem(i, held) * n_ten + ten) * half, half)
        here = i // held == ten

        @pl.when(here)
        def _(out=out, spot=spot):
            out[...] = mine[:, spot]

        @pl.when(jnp.logical_not(here))
        def _(out=out, spot=spot):
            out[...] = other[:, spot]


def kv_kernel(n_dp, where, *refs):
    pieces, (enc_mine, enc_other, out, grads) = refs[:n_dp], refs[n_dp:]
    tok = pieces[0].shape[0]
    half = enc_mine.shape[1]
    for k, piece in enumerate(pieces):
        grads[k * tok : (k + 1) * tok, :] = piece[...]
    for step, enc in ((0, enc_mine), (1, enc_other)):
        out[aligned((where[2] ^ step) * half, half), :] = lax.dot_general(
            enc[...], grads[...], (((0,), (0,)), ((), ())), preferred_element_type=F32
        ).astype(out.dtype)


def on_device(
    enc_out, mlp_input, grad_kv, kv_weight, gate_weight, up_weight, down_weight, norm_gain
):
    n_dp, n_pipe, n_ten = (lax.axis_size(a) for a in (DP, PIPE, TENSOR))
    tok = grad_kv.shape[0]
    width = norm_gain.shape[0]
    cols = kv_weight.shape[0]
    units = gate_weight.shape[1]
    share = cols // (n_pipe * n_ten)
    if (n_dp, n_pipe, n_ten) != (4, 4, 2) or share % 128 or tok % 128 or units % 128:
        return on_device_any(
            enc_out, mlp_input, grad_kv, kv_weight, gate_weight, up_weight, down_weight, norm_gain
        )
    where = jnp.stack([lax.axis_index(a) for a in (DP, PIPE, TENSOR)]).astype(jnp.int32)

    far, near = send(down_weight, PIPE, 2), send(down_weight, PIPE, 1)
    grads = gather(grad_kv.reshape(tok, -1), DP)
    x_other = send(mlp_input, TENSOR, 1)
    (both,) = call(
        pack_kernel, "gate_and_up", [shaped((2 * cols, units), BF16)], [where, gate_weight, up_weight]
    )
    grads, both = lax.optimization_barrier((grads, both))
    packs = gather(both, DP)
    grads, far, near = lax.optimization_barrier((grads, far, near))
    downs = [down_weight, near, far, send(far, PIPE, 1)]

    section = kv_weight.reshape(cols, -1)
    half = cols // n_ten
    (mine,) = call(
        lambda *refs: upstream_kernel(n_dp, *refs),
        "upstream_terms",
        [shaped((n_dp * tok, cols), BF16)],
        [where, *grads, section],
        [pltpu.VMEM((n_dp * tok, section.shape[1]), BF16)],
        flops=2 * n_dp * tok * section.size,
    )
    other = send(mine, TENSOR, 1)
    other, packs[1], packs[2] = lax.optimization_barrier((other, packs[1], packs[2]))
    group = n_pipe * units
    hidden, upstream, *outs = call(
        lambda *refs: hidden_kernel(n_dp, n_pipe, n_ten, *refs),
        "hidden_terms",
        [shaped((tok, group), F32), shaped((tok, half), BF16)]
        + [shaped((tok, group + half), BF16)] * (n_dp - 1),
        [where, mine, other, *downs],
        [pltpu.VMEM((n_dp * tok, cols), BF16), pltpu.VMEM((group, cols), BF16)],
        flops=2 * n_dp * tok * cols * group,
    )
    ups = [send(out, DP, k) for k, out in enumerate(outs, 1)]
    encoded = [enc_out, send(enc_out, TENSOR, 1)]
    encoded = call(
        lambda *refs: encoded_kernel(n_dp, n_ten, *refs),
        "encoded_blocks",
        [shaped((tok, half), BF16), shaped((2 * tok, half), BF16), shaped((tok, half), BF16)],
        [where, *encoded],
    )
    ups, encoded = lax.optimization_barrier((ups, encoded))
    for part in ups:
        hidden = hidden + part[:, :group].astype(F32)
    terms = [hidden[:, :units]]
    terms += [send(hidden[:, k * units : (k + 1) * units].astype(BF16), PIPE, k) for k in range(1, n_pipe)]

    gain_row = norm_gain.reshape(1, width)
    resid, scale, pre = call(
        lambda *refs: forward_kernel(n_dp, *refs),
        "mlp_forward",
        [shaped((tok, width), BF16), shaped((tok, 128), F32), shaped((tok, 2 * units), F32)],
        [where, *packs, mlp_input, x_other, gain_row],
        [pltpu.VMEM((tok, width), BF16)],
        flops=4 * tok * width * units,
    )
    other, mine = call(
        lambda *refs: backward_kernel(n_dp, n_pipe, n_ten, *refs),
        "mlp_backward",
        [shaped((n_pipe, tok, n_dp * share), BF16), shaped((n_pipe, tok, n_dp * share), F32)],
        [where, *terms, upstream, *ups, *packs, pre, scale, resid, gain_row],
        flops=4 * tok * width * units,
    )
    mine = mine + send(other, TENSOR, 1).astype(F32)
    first = send(encoded[1], DP, 1)
    second = jnp.concatenate([encoded[2], first[tok:]], axis=0)
    mine, second = lax.optimization_barrier((mine, second))
    terms = [send(mine[k].astype(BF16), PIPE, k) for k in range(1, n_pipe)]
    second = send(second, DP, 2)
    part = mine[0]
    for term in terms:
        part = part + term.astype(F32)
    part = part.astype(BF16)
    part, second = lax.optimization_barrier((part, second))
    parts = gather(part, PIPE)

    mine_enc = jnp.concatenate([encoded[0], first[:tok], second], axis=0)
    (kv_grad,) = call(
        lambda *refs: kv_kernel(n_dp, *refs),
        "kv_grad",
        [shaped((cols, section.shape[1]), BF16)],
        [where, *grads, mine_enc, send(mine_enc, TENSOR, 1)],
        [pltpu.VMEM((n_dp * tok, section.shape[1]), BF16)],
        flops=2 * n_dp * tok * section.size,
    )
    kv_grad = kv_grad.reshape(kv_weight.shape)
    parts, kv_grad = lax.optimization_barrier((parts, kv_grad))
    parts = parts + [send(part, TENSOR, 1) for part in parts]
    (input_grad,) = call(
        lambda *refs: assemble_kernel(n_dp, n_pipe, n_ten, *refs),
        "input_grad",
        [shaped((tok, width), BF16)],
        [where, *parts],
    )
    return (input_grad, kv_grad)


def solution(mesh):
    placed = (
        P(DP, TENSOR),
        P(DP, TENSOR),
        P(DP, None, PIPE, TENSOR),
        P(DP, None, PIPE, TENSOR),
        P(DP, (PIPE, TENSOR)),
        P(DP, (PIPE, TENSOR)),
        P((PIPE, TENSOR), DP),
        P(),
    )
    return jax.shard_map(
        on_device,
        mesh=mesh,
        in_specs=placed,
        out_specs=(P(DP, None), P(DP, None, PIPE, TENSOR)),
        check_vma=False,
    )
```

```python
import math

import jax
import jax.numpy as jnp
from jax import lax
from jax.experimental import pallas as pl
from jax.experimental.pallas import tpu as pltpu
from jax.sharding import PartitionSpec as P

DP, PIPE, TENSOR = "dp", "pipe", "tensor"
BF16, F32 = jnp.bfloat16, jnp.float32


def gelu_parts(preact):
    factor = math.sqrt(2.0 / math.pi)
    tangent = jnp.tanh(factor * (preact + 0.044715 * preact * preact * preact))
    gelu_value = 0.5 * preact * (1.0 + tangent)
    gelu_slope = 0.5 * (1.0 + tangent) + 0.5 * preact * (1.0 - tangent * tangent) * factor * (
        1.0 + 3.0 * 0.044715 * preact * preact
    )
    return (gelu_value, gelu_slope)


def send(value, axis, step):
    if step == 0:
        return value
    size = lax.axis_size(axis)
    return lax.ppermute(value, axis, [(src, src ^ step) for src in range(size)])


def gather(value, axis):
    return [send(value, axis, step) for step in range(lax.axis_size(axis))]


def relayed(value, axis):
    far, near = send(value, axis, 2), send(value, axis, 1)
    return [value, near, far, send(far, axis, 1)]


def natural(parts, axis, dim):
    mine = lax.axis_index(axis)
    width = parts[0].shape[dim]
    shape = list(parts[0].shape)
    shape[dim] = width * len(parts)
    out = jnp.zeros(shape, parts[0].dtype)
    for step, part in enumerate(parts):
        out = lax.dynamic_update_slice_in_dim(out, part, (mine ^ step) * width, dim)
    return out


def block(value, axis, step, dim):
    width = value.shape[dim] // lax.axis_size(axis)
    start = (lax.axis_index(axis) ^ step) * width
    return lax.dynamic_slice_in_dim(value, start, width, dim)


def total(blocks, axis):
    out = blocks[0].astype(F32)
    for step in range(1, len(blocks)):
        out = out + send(blocks[step].astype(BF16), axis, step).astype(F32)
    return out


def dot_nt(left, right):
    return lax.dot_general(left, right, (((1,), (1,)), ((), ())), preferred_element_type=F32)


def on_device_any(
    enc_out, mlp_input, grad_kv, kv_weight, gate_weight, up_weight, down_weight, norm_gain
):
    n_dp, n_pipe, n_ten = (lax.axis_size(a) for a in (DP, PIPE, TENSOR))
    tok = grad_kv.shape[0]
    width = norm_gain.shape[0]
    cols = kv_weight.shape[0]
    units = gate_weight.shape[1]
    share = cols // (n_pipe * n_ten)

    grads = jnp.concatenate(gather(grad_kv.reshape(tok, -1), DP), axis=0)

    section = kv_weight.reshape(cols, -1)
    partial = dot_nt(grads, section)
    partial = total([block(partial, TENSOR, k, 1) for k in range(n_ten)], TENSOR)
    partial = total([block(partial, PIPE, k, 1) for k in range(n_pipe)], PIPE)
    partial = partial.astype(BF16).reshape(n_dp, tok, share)
    upstream = jnp.concatenate([send(partial[k], DP, k) for k in range(n_dp)], axis=1)

    down = jnp.concatenate([send(block(down_weight, TENSOR, k, 1), TENSOR, k) for k in range(n_ten)], axis=0)
    down = jnp.concatenate([send(block(down, PIPE, k, 1), PIPE, k) for k in range(n_pipe)], axis=0)
    down = jnp.concatenate(gather(down, DP), axis=1)
    hidden = dot_nt(upstream, down).reshape(tok, n_pipe, n_ten, units)
    hidden = total([hidden[:, :, k] for k in range(n_ten)], TENSOR)
    hidden_grad = total([hidden[:, k] for k in range(n_pipe)], PIPE)

    both = jnp.concatenate([gate_weight, up_weight], axis=1)
    both = jnp.concatenate(gather(both, DP), axis=0)
    resid = natural(gather(mlp_input, TENSOR), TENSOR, 1)
    resid = jnp.concatenate([block(resid, DP, k, 1) for k in range(n_dp)], axis=1)
    gain_row = jnp.concatenate([block(norm_gain, DP, k, 0) for k in range(n_dp)], axis=0).astype(F32)
    values_in = resid.astype(F32)
    row_scale = lax.rsqrt(jnp.mean(values_in * values_in, axis=1, keepdims=True) + 1e-06)
    normed = (values_in * row_scale * gain_row).astype(BF16)
    pre = jnp.dot(normed, both, preferred_element_type=F32)
    gate_pre, up_pre = pre[:, :units], pre[:, units:]

    gelu_value, gelu_slope = gelu_parts(gate_pre)
    gate_grad = hidden_grad * up_pre * gelu_slope
    up_grad = hidden_grad * gelu_value
    dotted = jnp.sum(gate_grad * gate_pre + up_grad * up_pre, axis=1, keepdims=True)
    grads_both = jnp.concatenate([gate_grad, up_grad], axis=1).astype(BF16)
    normed_part = dot_nt(grads_both, both)
    part = row_scale * gain_row * normed_part - values_in * (row_scale * row_scale * (dotted / width))

    part = part.reshape(tok, n_dp, cols)
    part = total([block(part, TENSOR, k, 2) for k in range(n_ten)], TENSOR)
    part = total([block(part, PIPE, k, 2) for k in range(n_pipe)], PIPE)
    part = (part + upstream.reshape(tok, n_dp, share).astype(F32)).astype(BF16)
    whole = natural(gather(part, PIPE), PIPE, 2)
    whole = natural(gather(whole, TENSOR), TENSOR, 2)
    input_grad = natural([whole[:, k] for k in range(n_dp)], DP, 1)

    encoded = natural(gather(enc_out, TENSOR), TENSOR, 1)
    mine = [send(block(block(encoded, DP, k, 1), TENSOR, 0, 1), DP, k) for k in range(n_dp)]
    mine = jnp.concatenate(mine, axis=0)
    mine = natural(gather(mine, TENSOR), TENSOR, 1)
    kv_grad = lax.dot_general(
        mine, grads, (((0,), (0,)), ((), ())), preferred_element_type=F32
    ).astype(BF16)
    return (input_grad, kv_grad.reshape(kv_weight.shape))


def aligned(start, lanes):
    return pl.ds(pl.multiple_of(start, lanes), lanes)


def call(body, name, out, operands, scratch=(), flops=0):
    specs = [pl.BlockSpec(memory_space=pltpu.SMEM)]
    specs += [pl.BlockSpec(memory_space=pltpu.VMEM)] * (len(operands) - 1)
    moved = sum(a.size * a.dtype.itemsize for a in (*operands, *out))
    return pl.pallas_call(
        body,
        name=name,
        out_shape=out,
        in_specs=specs,
        out_specs=[pl.BlockSpec(memory_space=pltpu.VMEM)] * len(out),
        scratch_shapes=list(scratch),
        compiler_params=pltpu.CompilerParams(vmem_limit_bytes=40 * 1024 * 1024),
        cost_estimate=pl.CostEstimate(flops=flops, bytes_accessed=moved, transcendentals=0),
    )(*operands)


def shaped(shape, dtype):
    return jax.ShapeDtypeStruct(shape, dtype)


def pack_kernel(where, gate, up, out):
    cols = gate.shape[0]
    out[:cols, :] = gate[...]
    out[cols:, :] = up[...]


def upstream_kernel(n_dp, where, *refs):
    pieces, (section, out, grads) = refs[:n_dp], refs[n_dp:]
    tok = pieces[0].shape[0]
    for k, piece in enumerate(pieces):
        grads[k * tok : (k + 1) * tok, :] = piece[...]
    out[...] = dot_nt(grads[...], section[...]).astype(out.dtype)


def hidden_kernel(n_dp, n_pipe, n_ten, where, mine, other, *refs):
    downs, hidden, outs = refs[:n_pipe], refs[n_pipe : 2 * n_pipe], refs[2 * n_pipe : 2 * n_pipe + n_dp]
    upstream, down = refs[-2:]
    upstream[...] = (mine[...].astype(F32) + other[...].astype(F32)).astype(BF16)
    units = downs[0].shape[0]
    for k, part in enumerate(downs):
        down[k * units : (k + 1) * units, :] = part[...]
    result = dot_nt(upstream[...], down[...])
    for k, out in enumerate(hidden):
        out[...] = result[:, k * units : (k + 1) * units].astype(out.dtype)
    tok, half = outs[0].shape
    for k, out in enumerate(outs):
        out[...] = upstream[k * tok : (k + 1) * tok, aligned(where[2] * half, half)]


def owner_kernel(n_dp, n_pipe, where, *refs):
    terms, ups, own, outs = refs[:n_pipe], refs[n_pipe : n_pipe + n_dp - 1], refs[-n_dp], refs[1 - n_dp :]
    tok, units = own.shape
    for k in range(n_dp):
        total_here = terms[0][k * tok : (k + 1) * tok, :]
        for term in terms[1:]:
            total_here = total_here + term[k * tok : (k + 1) * tok, :].astype(F32)
        if k == 0:
            own[...] = total_here
        else:
            outs[k - 1][:, :units] = total_here.astype(BF16)
            outs[k - 1][:, units:] = ups[k - 1][...]


def gate_and_up(packs, k, cols, start, rows):
    if k < len(packs) - 2:
        pieces = [packs[k][aligned(s * cols + start, rows), :] for s in (0, 1)]
    else:
        pieces = [pack[aligned(start, rows), :] for pack in packs[-2:]]
    return jnp.concatenate(pieces, axis=1)


def forward_kernel(n_dp, where, *refs):
    packs, (x_mine, x_other, gain, resid, scale, pre, normed) = refs[: n_dp + 1], refs[n_dp + 1 :]
    ten = where[2]
    half = x_mine.shape[1]
    resid[:, aligned(ten * half, half)] = x_mine[...]
    resid[:, aligned((ten ^ 1) * half, half)] = x_other[...]
    values_in = resid[...].astype(F32)
    row_scale = lax.rsqrt(jnp.mean(values_in * values_in, axis=1, keepdims=True) + 1e-06)
    scale[...] = jnp.broadcast_to(row_scale, scale.shape)
    normed[...] = (values_in * row_scale * gain[...].astype(F32)).astype(BF16)
    cols = resid.shape[1] // n_dp
    result = jnp.zeros(pre.shape, F32)
    for k in range(n_dp):
        left = normed[:, aligned((where[0] ^ k) * cols, cols)]
        result += jnp.dot(left, gate_and_up(packs, k, cols, 0, cols), preferred_element_type=F32)
    pre[...] = result


def backward_kernel(n_dp, n_pipe, n_ten, where, *refs):
    terms, upstream, rest = refs[:n_dp], refs[n_dp], refs[n_dp + 1 :]
    units = terms[0].shape[1]
    ups = [upstream] + [term.at[:, units:] for term in terms[1:]]
    packs, (pre, scale, resid, gain, other, mine) = rest[: n_dp + 1], rest[n_dp + 1 :]
    pipe, ten = where[1], where[2]
    hidden_grad = terms[0][...]
    for term in terms[1:]:
        hidden_grad = hidden_grad + term[:, :units].astype(F32)
    gate_pre, up_pre = pre[:, :units], pre[:, units:]
    gelu_value, gelu_slope = gelu_parts(gate_pre)
    gate_grad = hidden_grad * up_pre * gelu_slope
    up_grad = hidden_grad * gelu_value
    dotted = jnp.sum(gate_grad * gate_pre + up_grad * up_pre, axis=1, keepdims=True)
    grads = jnp.concatenate([gate_grad, up_grad], axis=1).astype(BF16)
    row_scale = scale[:, :1]
    width = resid.shape[1]
    pull = row_scale * row_scale * (dotted / width)
    cols = width // n_dp
    half = cols // n_ten
    share = half // n_pipe
    for step, out in ((1, other), (0, mine)):
        start = (ten ^ step) * half
        for k in range(n_dp):
            i = where[0] ^ k
            spot = aligned(i * cols + start, half)
            part = dot_nt(grads, gate_and_up(packs, k, cols, start, half))
            part = row_scale * (gain[:, spot].astype(F32) * part) - resid[:, spot].astype(F32) * pull
            if step == 0:
                part = part + ups[k][...].astype(F32)
            part = part.astype(out.dtype)
            for j in range(n_pipe):
                out[pipe ^ j, :, aligned(i * share, share)] = part[:, j * share : (j + 1) * share]


def assemble_kernel(n_dp, n_pipe, n_ten, where, *refs):
    parts, out = refs[:-1], refs[-1]
    pipe, ten = where[1], where[2]
    share = parts[0].shape[1] // n_dp
    for core in range(n_ten):
        for k in range(n_pipe):
            part = parts[core * n_pipe + k]
            for i in range(n_dp):
                start = ((i * n_ten + (ten ^ core)) * n_pipe + (pipe ^ k)) * share
                out[:, aligned(start, share)] = part[:, i * share : (i + 1) * share]


def encoded_kernel(n_dp, n_ten, where, mine, other, own, near, far):
    dp, ten = where[0], where[2]
    tok, half = own.shape
    held = n_dp // n_ten
    for k, out in ((0, own), (1, near.at[:tok]), (3, near.at[tok:]), (2, far)):
        i = dp ^ k
        spot = aligned((lax.rem(i, held) * n_ten + ten) * half, half)
        here = i // held == ten

        @pl.when(here)
        def _(out=out, spot=spot):
            out[...] = mine[:, spot]

        @pl.when(jnp.logical_not(here))
        def _(out=out, spot=spot):
            out[...] = other[:, spot]


def kv_kernel(n_dp, where, *refs):
    pieces, (enc_mine, enc_other, out, grads) = refs[:n_dp], refs[n_dp:]
    tok = pieces[0].shape[0]
    half = enc_mine.shape[1]
    for k, piece in enumerate(pieces):
        grads[k * tok : (k + 1) * tok, :] = piece[...]
    for step, enc in ((0, enc_mine), (1, enc_other)):
        out[aligned((where[2] ^ step) * half, half), :] = lax.dot_general(
            enc[...], grads[...], (((0,), (0,)), ((), ())), preferred_element_type=F32
        ).astype(out.dtype)


def on_device(
    enc_out, mlp_input, grad_kv, kv_weight, gate_weight, up_weight, down_weight, norm_gain
):
    n_dp, n_pipe, n_ten = (lax.axis_size(a) for a in (DP, PIPE, TENSOR))
    tok = grad_kv.shape[0]
    width = norm_gain.shape[0]
    cols = kv_weight.shape[0]
    units = gate_weight.shape[1]
    share = cols // (n_pipe * n_ten)
    if (n_dp, n_pipe, n_ten) != (4, 4, 2) or share % 128 or tok % 128 or units % 128:
        return on_device_any(
            enc_out, mlp_input, grad_kv, kv_weight, gate_weight, up_weight, down_weight, norm_gain
        )
    where = jnp.stack([lax.axis_index(a) for a in (DP, PIPE, TENSOR)]).astype(jnp.int32)

    grads = gather(grad_kv.reshape(tok, -1), DP)
    x_other = send(mlp_input, TENSOR, 1)
    far, near = send(down_weight, PIPE, 2), send(down_weight, PIPE, 1)
    (both,) = call(
        pack_kernel, "gate_and_up", [shaped((2 * cols, units), BF16)], [where, gate_weight, up_weight]
    )
    grads, both = lax.optimization_barrier((grads, both))
    packs = [both, send(both, DP, 1), send(both, DP, 2)]
    grads, far, near = lax.optimization_barrier((grads, far, near))
    downs = [down_weight, near, far, send(far, PIPE, 1)]

    section = kv_weight.reshape(cols, -1)
    half = cols // n_ten
    (mine,) = call(
        lambda *refs: upstream_kernel(n_dp, *refs),
        "upstream_terms",
        [shaped((n_dp * tok, cols), BF16)],
        [where, *grads, section],
        [pltpu.VMEM((n_dp * tok, section.shape[1]), BF16)],
        flops=2 * n_dp * tok * section.size,
    )
    other = send(mine, TENSOR, 1)
    enc_other = send(enc_out, TENSOR, 1)
    other, x_other, enc_other = lax.optimization_barrier((other, x_other, enc_other))
    group = n_pipe * units
    outs = call(
        lambda *refs: hidden_kernel(n_dp, n_pipe, n_ten, *refs),
        "hidden_terms",
        [shaped((n_dp * tok, units), F32)]
        + [shaped((n_dp * tok, units), BF16)] * (n_pipe - 1)
        + [shaped((tok, half), BF16)] * n_dp,
        [where, mine, other, *downs],
        [pltpu.VMEM((n_dp * tok, cols), BF16), pltpu.VMEM((group, cols), BF16)],
        flops=2 * n_dp * tok * cols * group,
    )
    terms = [send(out, PIPE, k) for k, out in enumerate(outs[:n_pipe])]
    packs = lax.optimization_barrier((terms[1], packs))[1]
    packs += [send(packs[1][:cols], DP, 2), send(packs[2][cols:], DP, 1)]
    hidden, *ups = call(
        lambda *refs: owner_kernel(n_dp, n_pipe, *refs),
        "hidden_sums",
        [shaped((tok, units), F32)] + [shaped((tok, units + half), BF16)] * (n_dp - 1),
        [where, *terms, *outs[n_pipe + 1 :]],
    )
    terms = [hidden] + [send(up, DP, k) for k, up in enumerate(ups, 1)]
    encoded = [enc_out, enc_other]
    encoded = call(
        lambda *refs: encoded_kernel(n_dp, n_ten, *refs),
        "encoded_blocks",
        [shaped((tok, half), BF16), shaped((2 * tok, half), BF16), shaped((tok, half), BF16)],
        [where, *encoded],
    )
    terms, encoded = lax.optimization_barrier((terms, encoded))

    gain_row = norm_gain.reshape(1, width)
    resid, scale, pre = call(
        lambda *refs: forward_kernel(n_dp, *refs),
        "mlp_forward",
        [shaped((tok, width), BF16), shaped((tok, 128), F32), shaped((tok, 2 * units), F32)],
        [where, *packs, mlp_input, x_other, gain_row],
        [pltpu.VMEM((tok, width), BF16)],
        flops=4 * tok * width * units,
    )
    other, mine = call(
        lambda *refs: backward_kernel(n_dp, n_pipe, n_ten, *refs),
        "mlp_backward",
        [shaped((n_pipe, tok, n_dp * share), BF16), shaped((n_pipe, tok, n_dp * share), F32)],
        [where, *terms, outs[n_pipe], *packs, pre, scale, resid, gain_row],
        flops=4 * tok * width * units,
    )
    mine = mine + send(other, TENSOR, 1).astype(F32)
    first = send(encoded[1], DP, 1)
    second = jnp.concatenate([encoded[2], first[tok:]], axis=0)
    mine, second = lax.optimization_barrier((mine, second))
    terms = [send(mine[k].astype(BF16), PIPE, k) for k in range(1, n_pipe)]
    second = send(second, DP, 2)
    part = mine[0]
    for term in terms:
        part = part + term.astype(F32)
    part = part.astype(BF16)
    part, second = lax.optimization_barrier((part, second))
    parts = gather(part, PIPE)

    mine_enc = jnp.concatenate([encoded[0], first[:tok], second], axis=0)
    (kv_grad,) = call(
        lambda *refs: kv_kernel(n_dp, *refs),
        "kv_grad",
        [shaped((cols, section.shape[1]), BF16)],
        [where, *grads, mine_enc, send(mine_enc, TENSOR, 1)],
        [pltpu.VMEM((n_dp * tok, section.shape[1]), BF16)],
        flops=2 * n_dp * tok * section.size,
    )
    kv_grad = kv_grad.reshape(kv_weight.shape)
    parts, kv_grad = lax.optimization_barrier((parts, kv_grad))
    parts = parts + [send(part, TENSOR, 1) for part in parts]
    (input_grad,) = call(
        lambda *refs: assemble_kernel(n_dp, n_pipe, n_ten, *refs),
        "input_grad",
        [shaped((tok, width), BF16)],
        [where, *parts],
    )
    return (input_grad, kv_grad)


def solution(mesh):
    placed = (
        P(DP, TENSOR),
        P(DP, TENSOR),
        P(DP, None, PIPE, TENSOR),
        P(DP, None, PIPE, TENSOR),
        P(DP, (PIPE, TENSOR)),
        P(DP, (PIPE, TENSOR)),
        P((PIPE, TENSOR), DP),
        P(),
    )
    return jax.shard_map(
        on_device,
        mesh=mesh,
        in_specs=placed,
        out_specs=(P(DP, None), P(DP, None, PIPE, TENSOR)),
        check_vma=False,
    )
```

```python
import math

import jax
import jax.numpy as jnp
from jax import lax
from jax.experimental import pallas as pl
from jax.experimental.pallas import tpu as pltpu
from jax.sharding import PartitionSpec as P

DP, PIPE, TENSOR = "dp", "pipe", "tensor"
BF16, F32 = jnp.bfloat16, jnp.float32


def gelu_parts(preact):
    factor = math.sqrt(2.0 / math.pi)
    tangent = jnp.tanh(factor * (preact + 0.044715 * preact * preact * preact))
    gelu_value = 0.5 * preact * (1.0 + tangent)
    gelu_slope = 0.5 * (1.0 + tangent) + 0.5 * preact * (1.0 - tangent * tangent) * factor * (
        1.0 + 3.0 * 0.044715 * preact * preact
    )
    return (gelu_value, gelu_slope)


def send(value, axis, step):
    if step == 0:
        return value
    size = lax.axis_size(axis)
    return lax.ppermute(value, axis, [(src, src ^ step) for src in range(size)])


def gather(value, axis):
    return [send(value, axis, step) for step in range(lax.axis_size(axis))]


def relayed(value, axis):
    far, near = send(value, axis, 2), send(value, axis, 1)
    return [value, near, far, send(far, axis, 1)]


def natural(parts, axis, dim):
    mine = lax.axis_index(axis)
    width = parts[0].shape[dim]
    shape = list(parts[0].shape)
    shape[dim] = width * len(parts)
    out = jnp.zeros(shape, parts[0].dtype)
    for step, part in enumerate(parts):
        out = lax.dynamic_update_slice_in_dim(out, part, (mine ^ step) * width, dim)
    return out


def block(value, axis, step, dim):
    width = value.shape[dim] // lax.axis_size(axis)
    start = (lax.axis_index(axis) ^ step) * width
    return lax.dynamic_slice_in_dim(value, start, width, dim)


def total(blocks, axis):
    out = blocks[0].astype(F32)
    for step in range(1, len(blocks)):
        out = out + send(blocks[step].astype(BF16), axis, step).astype(F32)
    return out


def dot_nt(left, right):
    return lax.dot_general(left, right, (((1,), (1,)), ((), ())), preferred_element_type=F32)


def on_device_any(
    enc_out, mlp_input, grad_kv, kv_weight, gate_weight, up_weight, down_weight, norm_gain
):
    n_dp, n_pipe, n_ten = (lax.axis_size(a) for a in (DP, PIPE, TENSOR))
    tok = grad_kv.shape[0]
    width = norm_gain.shape[0]
    cols = kv_weight.shape[0]
    units = gate_weight.shape[1]
    share = cols // (n_pipe * n_ten)

    grads = jnp.concatenate(gather(grad_kv.reshape(tok, -1), DP), axis=0)

    section = kv_weight.reshape(cols, -1)
    partial = dot_nt(grads, section)
    partial = total([block(partial, TENSOR, k, 1) for k in range(n_ten)], TENSOR)
    partial = total([block(partial, PIPE, k, 1) for k in range(n_pipe)], PIPE)
    partial = partial.astype(BF16).reshape(n_dp, tok, share)
    upstream = jnp.concatenate([send(partial[k], DP, k) for k in range(n_dp)], axis=1)

    down = jnp.concatenate([send(block(down_weight, TENSOR, k, 1), TENSOR, k) for k in range(n_ten)], axis=0)
    down = jnp.concatenate([send(block(down, PIPE, k, 1), PIPE, k) for k in range(n_pipe)], axis=0)
    down = jnp.concatenate(gather(down, DP), axis=1)
    hidden = dot_nt(upstream, down).reshape(tok, n_pipe, n_ten, units)
    hidden = total([hidden[:, :, k] for k in range(n_ten)], TENSOR)
    hidden_grad = total([hidden[:, k] for k in range(n_pipe)], PIPE)

    both = jnp.concatenate([gate_weight, up_weight], axis=1)
    both = jnp.concatenate(gather(both, DP), axis=0)
    resid = natural(gather(mlp_input, TENSOR), TENSOR, 1)
    resid = jnp.concatenate([block(resid, DP, k, 1) for k in range(n_dp)], axis=1)
    gain_row = jnp.concatenate([block(norm_gain, DP, k, 0) for k in range(n_dp)], axis=0).astype(F32)
    values_in = resid.astype(F32)
    row_scale = lax.rsqrt(jnp.mean(values_in * values_in, axis=1, keepdims=True) + 1e-06)
    normed = (values_in * row_scale * gain_row).astype(BF16)
    pre = jnp.dot(normed, both, preferred_element_type=F32)
    gate_pre, up_pre = pre[:, :units], pre[:, units:]

    gelu_value, gelu_slope = gelu_parts(gate_pre)
    gate_grad = hidden_grad * up_pre * gelu_slope
    up_grad = hidden_grad * gelu_value
    dotted = jnp.sum(gate_grad * gate_pre + up_grad * up_pre, axis=1, keepdims=True)
    grads_both = jnp.concatenate([gate_grad, up_grad], axis=1).astype(BF16)
    normed_part = dot_nt(grads_both, both)
    part = row_scale * gain_row * normed_part - values_in * (row_scale * row_scale * (dotted / width))

    part = part.reshape(tok, n_dp, cols)
    part = total([block(part, TENSOR, k, 2) for k in range(n_ten)], TENSOR)
    part = total([block(part, PIPE, k, 2) for k in range(n_pipe)], PIPE)
    part = (part + upstream.reshape(tok, n_dp, share).astype(F32)).astype(BF16)
    whole = natural(gather(part, PIPE), PIPE, 2)
    whole = natural(gather(whole, TENSOR), TENSOR, 2)
    input_grad = natural([whole[:, k] for k in range(n_dp)], DP, 1)

    encoded = natural(gather(enc_out, TENSOR), TENSOR, 1)
    mine = [send(block(block(encoded, DP, k, 1), TENSOR, 0, 1), DP, k) for k in range(n_dp)]
    mine = jnp.concatenate(mine, axis=0)
    mine = natural(gather(mine, TENSOR), TENSOR, 1)
    kv_grad = lax.dot_general(
        mine, grads, (((0,), (0,)), ((), ())), preferred_element_type=F32
    ).astype(BF16)
    return (input_grad, kv_grad.reshape(kv_weight.shape))


def aligned(start, lanes):
    return pl.ds(pl.multiple_of(start, lanes), lanes)


def call(body, name, out, operands, scratch=(), flops=0, space=pltpu.VMEM):
    specs = [pl.BlockSpec(memory_space=pltpu.SMEM)]
    specs += [pl.BlockSpec(memory_space=pltpu.VMEM)] * (len(operands) - 1)
    moved = sum(a.size * a.dtype.itemsize for a in (*operands, *out))
    return pl.pallas_call(
        body,
        name=name,
        out_shape=out,
        in_specs=specs,
        out_specs=[pl.BlockSpec(memory_space=space)] * len(out),
        scratch_shapes=list(scratch),
        compiler_params=pltpu.CompilerParams(vmem_limit_bytes=40 * 1024 * 1024),
        cost_estimate=pl.CostEstimate(flops=flops, bytes_accessed=moved, transcendentals=0),
    )(*operands)


def shaped(shape, dtype):
    return jax.ShapeDtypeStruct(shape, dtype)


def upstream_kernel(n_dp, where, *refs):
    pieces, (section, out, grads) = refs[:n_dp], refs[n_dp:]
    tok = pieces[0].shape[0]
    for k, piece in enumerate(pieces):
        grads[k * tok : (k + 1) * tok, :] = piece[...]
    out[...] = dot_nt(grads[...], section[...]).astype(out.dtype)


def hidden_kernel(n_dp, n_pipe, n_ten, where, mine, other, *refs):
    downs, hidden, outs = refs[:n_pipe], refs[n_pipe : 2 * n_pipe], refs[2 * n_pipe : 2 * n_pipe + n_dp]
    upstream, down = refs[-2:]
    upstream[...] = (mine[...].astype(F32) + other[...].astype(F32)).astype(BF16)
    units = downs[0].shape[0]
    for k, part in enumerate(downs):
        down[k * units : (k + 1) * units, :] = part[...]
    result = dot_nt(upstream[...], down[...])
    for k, out in enumerate(hidden):
        out[...] = result[:, k * units : (k + 1) * units].astype(out.dtype)
    tok, half = outs[0].shape
    for k, out in enumerate(outs):
        out[...] = upstream[k * tok : (k + 1) * tok, aligned(where[2] * half, half)]


def owner_kernel(n_dp, n_pipe, where, *refs):
    terms, ups, own, outs = refs[:n_pipe], refs[n_pipe : n_pipe + n_dp - 1], refs[-n_dp], refs[1 - n_dp :]
    tok, units = own.shape
    for k in range(n_dp):
        total_here = terms[0][k * tok : (k + 1) * tok, :]
        for term in terms[1:]:
            total_here = total_here + term[k * tok : (k + 1) * tok, :].astype(F32)
        if k == 0:
            own[...] = total_here
        else:
            outs[k - 1][:, :units] = total_here.astype(BF16)
            outs[k - 1][:, units:] = ups[k - 1][...]


def gate_and_up(packs, k, start, rows):
    pieces = [pack[aligned(start, rows), :] for pack in (packs[k], packs[len(packs) // 2 + k])]
    return jnp.concatenate(pieces, axis=1)


def forward_kernel(n_dp, where, *refs):
    packs, (x_mine, x_other, gain, resid, scale, pre, last, normed) = refs[: 2 * (n_dp - 1)], refs[2 * (n_dp - 1) :]
    ten = where[2]
    half = x_mine.shape[1]
    resid[:, aligned(ten * half, half)] = x_mine[...]
    resid[:, aligned((ten ^ 1) * half, half)] = x_other[...]
    values_in = resid[...].astype(F32)
    row_scale = lax.rsqrt(jnp.mean(values_in * values_in, axis=1, keepdims=True) + 1e-06)
    scale[...] = jnp.broadcast_to(row_scale, scale.shape)
    normed[...] = (values_in * row_scale * gain[...].astype(F32)).astype(BF16)
    cols = resid.shape[1] // n_dp
    result = jnp.zeros(pre.shape, F32)
    for k in range(n_dp - 1):
        left = normed[:, aligned((where[0] ^ k) * cols, cols)]
        result += jnp.dot(left, gate_and_up(packs, k, 0, cols), preferred_element_type=F32)
    last[...] = normed[:, aligned((where[0] ^ (n_dp - 1)) * cols, cols)]
    pre[...] = result


def backward_kernel(n_dp, n_pipe, n_ten, where, *refs):
    terms, upstream, rest = refs[:n_dp], refs[n_dp], refs[n_dp + 1 :]
    units = terms[0].shape[1]
    ups = [upstream] + [term.at[:, units:] for term in terms[1:]]
    packs, (pre, last, scale, resid, gain, other, mine) = rest[: 2 * n_dp], rest[2 * n_dp :]
    pipe, ten = where[1], where[2]
    hidden_grad = terms[0][...]
    for term in terms[1:]:
        hidden_grad = hidden_grad + term[:, :units].astype(F32)
    both = gate_and_up(packs, n_dp - 1, 0, last.shape[1])
    pre_here = pre[...] + jnp.dot(last[...], both, preferred_element_type=F32)
    gate_pre, up_pre = pre_here[:, :units], pre_here[:, units:]
    gelu_value, gelu_slope = gelu_parts(gate_pre)
    gate_grad = hidden_grad * up_pre * gelu_slope
    up_grad = hidden_grad * gelu_value
    dotted = jnp.sum(gate_grad * gate_pre + up_grad * up_pre, axis=1, keepdims=True)
    grads = jnp.concatenate([gate_grad, up_grad], axis=1).astype(BF16)
    row_scale = scale[:, :1]
    width = resid.shape[1]
    pull = row_scale * row_scale * (dotted / width)
    cols = width // n_dp
    half = cols // n_ten
    share = half // n_pipe
    for step, out in ((1, other), (0, mine)):
        start = (ten ^ step) * half
        for k in range(n_dp):
            i = where[0] ^ k
            spot = aligned(i * cols + start, half)
            part = dot_nt(grads, gate_and_up(packs, k, start, half))
            part = row_scale * (gain[:, spot].astype(F32) * part) - resid[:, spot].astype(F32) * pull
            if step == 0:
                part = part + ups[k][...].astype(F32)
            part = part.astype(out.dtype)
            for j in range(n_pipe):
                out[pipe ^ j, :, aligned(i * share, share)] = part[:, j * share : (j + 1) * share]


def assemble_kernel(n_dp, n_pipe, n_ten, where, *refs):
    parts, (out, held, sems) = refs[:-3], refs[-3:]
    pipe, ten = where[1], where[2]
    share = parts[0].shape[1] // n_dp
    width = share * n_pipe
    copies = []
    for i in range(n_dp):
        for core in range(n_ten):
            at = i * n_ten + core
            for k in range(n_pipe):
                part = parts[core * n_pipe + k]
                held[at, :, aligned((pipe ^ k) * share, share)] = part[:, i * share : (i + 1) * share]
            spot = aligned((i * n_ten + (ten ^ core)) * width, width)
            copies.append(pltpu.make_async_copy(held.at[at], out.at[:, spot], sems.at[at]))
            copies[-1].start()
    for copy in copies:
        copy.wait()


def encoded_kernel(n_dp, n_ten, where, mine, other, own, near, far):
    dp, ten = where[0], where[2]
    tok, half = own.shape
    held = n_dp // n_ten
    for k, out in ((0, own), (1, near.at[:tok]), (3, near.at[tok:]), (2, far)):
        i = dp ^ k
        spot = aligned((lax.rem(i, held) * n_ten + ten) * half, half)
        here = i // held == ten

        @pl.when(here)
        def _(out=out, spot=spot):
            out[...] = mine[:, spot]

        @pl.when(jnp.logical_not(here))
        def _(out=out, spot=spot):
            out[...] = other[:, spot]


def kv_kernel(n_dp, where, *refs):
    pieces, (enc_mine, enc_other, out, grads) = refs[:n_dp], refs[n_dp:]
    tok = pieces[0].shape[0]
    half = enc_mine.shape[1]
    for k, piece in enumerate(pieces):
        grads[k * tok : (k + 1) * tok, :] = piece[...]
    for step, enc in ((0, enc_mine), (1, enc_other)):
        out[aligned((where[2] ^ step) * half, half), :] = lax.dot_general(
            enc[...], grads[...], (((0,), (0,)), ((), ())), preferred_element_type=F32
        ).astype(out.dtype)


def on_device(
    enc_out, mlp_input, grad_kv, kv_weight, gate_weight, up_weight, down_weight, norm_gain
):
    n_dp, n_pipe, n_ten = (lax.axis_size(a) for a in (DP, PIPE, TENSOR))
    tok = grad_kv.shape[0]
    width = norm_gain.shape[0]
    cols = kv_weight.shape[0]
    units = gate_weight.shape[1]
    share = cols // (n_pipe * n_ten)
    if (n_dp, n_pipe, n_ten) != (4, 4, 2) or share % 128 or tok % 128 or units % 128:
        return on_device_any(
            enc_out, mlp_input, grad_kv, kv_weight, gate_weight, up_weight, down_weight, norm_gain
        )
    where = jnp.stack([lax.axis_index(a) for a in (DP, PIPE, TENSOR)]).astype(jnp.int32)

    grads = gather(grad_kv.reshape(tok, -1), DP)
    x_other = send(mlp_input, TENSOR, 1)
    far, near = send(down_weight, PIPE, 2), send(down_weight, PIPE, 1)
    grads, gate, up = lax.optimization_barrier((grads, gate_weight, up_weight))
    gates, ups = [[value] + [send(value, DP, k) for k in (1, 2)] for value in (gate, up)]
    grads, far, near = lax.optimization_barrier((grads, far, near))
    downs = [down_weight, near, far, send(far, PIPE, 1)]

    section = kv_weight.reshape(cols, -1)
    half = cols // n_ten
    (mine,) = call(
        lambda *refs: upstream_kernel(n_dp, *refs),
        "upstream_terms",
        [shaped((n_dp * tok, cols), BF16)],
        [where, *grads, section],
        [pltpu.VMEM((n_dp * tok, section.shape[1]), BF16)],
        flops=2 * n_dp * tok * section.size,
    )
    other = send(mine, TENSOR, 1)
    enc_other = send(enc_out, TENSOR, 1)
    other, x_other, enc_other = lax.optimization_barrier((other, x_other, enc_other))
    group = n_pipe * units
    outs = call(
        lambda *refs: hidden_kernel(n_dp, n_pipe, n_ten, *refs),
        "hidden_terms",
        [shaped((n_dp * tok, units), F32)]
        + [shaped((n_dp * tok, units), BF16)] * (n_pipe - 1)
        + [shaped((tok, half), BF16)] * n_dp,
        [where, mine, other, *downs],
        [pltpu.VMEM((n_dp * tok, cols), BF16), pltpu.VMEM((group, cols), BF16)],
        flops=2 * n_dp * tok * cols * group,
    )
    terms = [send(out, PIPE, k) for k, out in enumerate(outs[:n_pipe])]
    gain_row = norm_gain.reshape(1, width)
    resid, scale, pre, last = call(
        lambda *refs: forward_kernel(n_dp, *refs),
        "mlp_forward",
        [shaped((tok, width), BF16), shaped((tok, 128), F32), shaped((tok, 2 * units), F32), shaped((tok, cols), BF16)],
        [where, *gates, *ups, mlp_input, x_other, gain_row],
        [pltpu.VMEM((tok, width), BF16)],
        flops=4 * tok * width * units,
    )
    packs = [*gates, send(gates[1], DP, 2), *ups, send(ups[2], DP, 1)]
    terms, resid, scale, pre, last = lax.optimization_barrier((terms, resid, scale, pre, last))
    hidden, *sums = call(
        lambda *refs: owner_kernel(n_dp, n_pipe, *refs),
        "hidden_sums",
        [shaped((tok, units), F32)] + [shaped((tok, units + half), BF16)] * (n_dp - 1),
        [where, *terms, *outs[n_pipe + 1 :]],
    )
    terms = [hidden] + [send(part, DP, k) for k, part in enumerate(sums, 1)]
    encoded = [enc_out, enc_other]
    encoded = call(
        lambda *refs: encoded_kernel(n_dp, n_ten, *refs),
        "encoded_blocks",
        [shaped((tok, half), BF16), shaped((2 * tok, half), BF16), shaped((tok, half), BF16)],
        [where, *encoded],
    )
    terms, encoded = lax.optimization_barrier((terms, encoded))

    other, mine = call(
        lambda *refs: backward_kernel(n_dp, n_pipe, n_ten, *refs),
        "mlp_backward",
        [shaped((n_pipe, tok, n_dp * share), BF16), shaped((n_pipe, tok, n_dp * share), F32)],
        [where, *terms, outs[n_pipe], *packs, pre, last, scale, resid, gain_row],
        flops=4 * tok * width * units,
    )
    mine = mine + send(other, TENSOR, 1).astype(F32)
    first = send(encoded[1], DP, 1)
    second = jnp.concatenate([encoded[2], first[tok:]], axis=0)
    mine, second = lax.optimization_barrier((mine, second))
    terms = [send(mine[k].astype(BF16), PIPE, k) for k in range(1, n_pipe)]
    second = send(second, DP, 2)
    part = mine[0]
    for term in terms:
        part = part + term.astype(F32)
    part = part.astype(BF16)
    part, second = lax.optimization_barrier((part, second))
    parts = gather(part, PIPE)

    mine_enc = jnp.concatenate([encoded[0], first[:tok], second], axis=0)
    (kv_grad,) = call(
        lambda *refs: kv_kernel(n_dp, *refs),
        "kv_grad",
        [shaped((cols, section.shape[1]), BF16)],
        [where, *grads, mine_enc, send(mine_enc, TENSOR, 1)],
        [pltpu.VMEM((n_dp * tok, section.shape[1]), BF16)],
        flops=2 * n_dp * tok * section.size,
    )
    kv_grad = kv_grad.reshape(kv_weight.shape)
    swapped = send(part, TENSOR, 1)
    parts, swapped, kv_grad = lax.optimization_barrier((parts, swapped, kv_grad))
    parts = parts + [swapped] + [send(part, TENSOR, 1) for part in parts[1:]]
    (input_grad,) = call(
        lambda *refs: assemble_kernel(n_dp, n_pipe, n_ten, *refs),
        "input_grad",
        [shaped((tok, width), BF16)],
        [where, *parts],
        [
            pltpu.VMEM((n_dp * n_ten, tok, width // (n_dp * n_ten)), BF16),
            pltpu.SemaphoreType.DMA((n_dp * n_ten,)),
        ],
        space=pl.ANY,
    )
    return (input_grad, kv_grad)


def solution(mesh):
    placed = (
        P(DP, TENSOR),
        P(DP, TENSOR),
        P(DP, None, PIPE, TENSOR),
        P(DP, None, PIPE, TENSOR),
        P(DP, (PIPE, TENSOR)),
        P(DP, (PIPE, TENSOR)),
        P((PIPE, TENSOR), DP),
        P(),
    )
    return jax.shard_map(
        on_device,
        mesh=mesh,
        in_specs=placed,
        out_specs=(P(DP, None), P(DP, None, PIPE, TENSOR)),
        check_vma=False,
    )
```

```python
import functools
import math

import jax
import jax.numpy as jnp
from jax import lax
from jax.experimental import pallas as pl
from jax.experimental.pallas import tpu as pltpu
from jax.sharding import PartitionSpec as P

DP, PIPE, TENSOR = "dp", "pipe", "tensor"
BF16, F32 = jnp.bfloat16, jnp.float32


def gelu_parts(preact):
    factor = math.sqrt(2.0 / math.pi)
    tangent = jnp.tanh(factor * (preact + 0.044715 * preact * preact * preact))
    gelu_value = 0.5 * preact * (1.0 + tangent)
    gelu_slope = 0.5 * (1.0 + tangent) + 0.5 * preact * (1.0 - tangent * tangent) * factor * (
        1.0 + 3.0 * 0.044715 * preact * preact
    )
    return (gelu_value, gelu_slope)


def send(value, axis, step):
    if step == 0:
        return value
    size = lax.axis_size(axis)
    return lax.ppermute(value, axis, [(src, src ^ step) for src in range(size)])


def gather(value, axis):
    return [send(value, axis, step) for step in range(lax.axis_size(axis))]


def relayed(value, axis):
    far, near = send(value, axis, 2), send(value, axis, 1)
    return [value, near, far, send(far, axis, 1)]


def natural(parts, axis, dim):
    mine = lax.axis_index(axis)
    width = parts[0].shape[dim]
    shape = list(parts[0].shape)
    shape[dim] = width * len(parts)
    out = jnp.zeros(shape, parts[0].dtype)
    for step, part in enumerate(parts):
        out = lax.dynamic_update_slice_in_dim(out, part, (mine ^ step) * width, dim)
    return out


def block(value, axis, step, dim):
    width = value.shape[dim] // lax.axis_size(axis)
    start = (lax.axis_index(axis) ^ step) * width
    return lax.dynamic_slice_in_dim(value, start, width, dim)


def total(blocks, axis):
    out = blocks[0].astype(F32)
    for step in range(1, len(blocks)):
        out = out + send(blocks[step].astype(BF16), axis, step).astype(F32)
    return out


def dot_nt(left, right):
    return lax.dot_general(left, right, (((1,), (1,)), ((), ())), preferred_element_type=F32)


def on_device_any(
    enc_out, mlp_input, grad_kv, kv_weight, gate_weight, up_weight, down_weight, norm_gain
):
    n_dp, n_pipe, n_ten = (lax.axis_size(a) for a in (DP, PIPE, TENSOR))
    tok = grad_kv.shape[0]
    width = norm_gain.shape[0]
    cols = kv_weight.shape[0]
    units = gate_weight.shape[1]
    share = cols // (n_pipe * n_ten)

    grads = jnp.concatenate(gather(grad_kv.reshape(tok, -1), DP), axis=0)

    section = kv_weight.reshape(cols, -1)
    partial = dot_nt(grads, section)
    partial = total([block(partial, TENSOR, k, 1) for k in range(n_ten)], TENSOR)
    partial = total([block(partial, PIPE, k, 1) for k in range(n_pipe)], PIPE)
    partial = partial.astype(BF16).reshape(n_dp, tok, share)
    upstream = jnp.concatenate([send(partial[k], DP, k) for k in range(n_dp)], axis=1)

    down = jnp.concatenate([send(block(down_weight, TENSOR, k, 1), TENSOR, k) for k in range(n_ten)], axis=0)
    down = jnp.concatenate([send(block(down, PIPE, k, 1), PIPE, k) for k in range(n_pipe)], axis=0)
    down = jnp.concatenate(gather(down, DP), axis=1)
    hidden = dot_nt(upstream, down).reshape(tok, n_pipe, n_ten, units)
    hidden = total([hidden[:, :, k] for k in range(n_ten)], TENSOR)
    hidden_grad = total([hidden[:, k] for k in range(n_pipe)], PIPE)

    both = jnp.concatenate([gate_weight, up_weight], axis=1)
    both = jnp.concatenate(gather(both, DP), axis=0)
    resid = natural(gather(mlp_input, TENSOR), TENSOR, 1)
    resid = jnp.concatenate([block(resid, DP, k, 1) for k in range(n_dp)], axis=1)
    gain_row = jnp.concatenate([block(norm_gain, DP, k, 0) for k in range(n_dp)], axis=0).astype(F32)
    values_in = resid.astype(F32)
    row_scale = lax.rsqrt(jnp.mean(values_in * values_in, axis=1, keepdims=True) + 1e-06)
    normed = (values_in * row_scale * gain_row).astype(BF16)
    pre = jnp.dot(normed, both, preferred_element_type=F32)
    gate_pre, up_pre = pre[:, :units], pre[:, units:]

    gelu_value, gelu_slope = gelu_parts(gate_pre)
    gate_grad = hidden_grad * up_pre * gelu_slope
    up_grad = hidden_grad * gelu_value
    dotted = jnp.sum(gate_grad * gate_pre + up_grad * up_pre, axis=1, keepdims=True)
    grads_both = jnp.concatenate([gate_grad, up_grad], axis=1).astype(BF16)
    normed_part = dot_nt(grads_both, both)
    part = row_scale * gain_row * normed_part - values_in * (row_scale * row_scale * (dotted / width))

    part = part.reshape(tok, n_dp, cols)
    part = total([block(part, TENSOR, k, 2) for k in range(n_ten)], TENSOR)
    part = total([block(part, PIPE, k, 2) for k in range(n_pipe)], PIPE)
    part = (part + upstream.reshape(tok, n_dp, share).astype(F32)).astype(BF16)
    whole = natural(gather(part, PIPE), PIPE, 2)
    whole = natural(gather(whole, TENSOR), TENSOR, 2)
    input_grad = natural([whole[:, k] for k in range(n_dp)], DP, 1)

    encoded = natural(gather(enc_out, TENSOR), TENSOR, 1)
    mine = [send(block(block(encoded, DP, k, 1), TENSOR, 0, 1), DP, k) for k in range(n_dp)]
    mine = jnp.concatenate(mine, axis=0)
    mine = natural(gather(mine, TENSOR), TENSOR, 1)
    kv_grad = lax.dot_general(
        mine, grads, (((0,), (0,)), ((), ())), preferred_element_type=F32
    ).astype(BF16)
    return (input_grad, kv_grad.reshape(kv_weight.shape))


def aligned(start, lanes):
    return pl.ds(pl.multiple_of(start, lanes), lanes)


def call(body, name, out, operands, scratch=(), flops=0, space=pltpu.VMEM, onto=False):
    specs = [pl.BlockSpec(memory_space=pltpu.SMEM)]
    specs += [pl.BlockSpec(memory_space=pltpu.VMEM)] * (len(operands) - 1)
    if onto:
        specs[-1] = pl.BlockSpec(memory_space=space)
    moved = sum(a.size * a.dtype.itemsize for a in (*operands, *out))
    return pl.pallas_call(
        body,
        name=name,
        out_shape=out,
        in_specs=specs,
        out_specs=[pl.BlockSpec(memory_space=space)] * len(out),
        scratch_shapes=list(scratch),
        input_output_aliases={len(operands) - 1: 0} if onto else {},
        compiler_params=pltpu.CompilerParams(vmem_limit_bytes=40 * 1024 * 1024),
        cost_estimate=pl.CostEstimate(flops=flops, bytes_accessed=moved, transcendentals=0),
    )(*operands)


def shaped(shape, dtype):
    return jax.ShapeDtypeStruct(shape, dtype)


def upstream_kernel(n_dp, where, *refs):
    pieces, (section, out, grads) = refs[:n_dp], refs[n_dp:]
    tok = pieces[0].shape[0]
    for k, piece in enumerate(pieces):
        grads[k * tok : (k + 1) * tok, :] = piece[...]
    out[...] = dot_nt(grads[...], section[...]).astype(out.dtype)


def hidden_kernel(n_dp, n_pipe, n_ten, where, mine, other, *refs):
    downs, hidden, outs = refs[:n_pipe], refs[n_pipe : 2 * n_pipe], refs[2 * n_pipe : 2 * n_pipe + n_dp]
    upstream, down = refs[-2:]
    upstream[...] = (mine[...].astype(F32) + other[...].astype(F32)).astype(BF16)
    units = downs[0].shape[0]
    for k, part in enumerate(downs):
        down[k * units : (k + 1) * units, :] = part[...]
    result = dot_nt(upstream[...], down[...])
    for k, out in enumerate(hidden):
        out[...] = result[:, k * units : (k + 1) * units].astype(out.dtype)
    tok, half = outs[0].shape
    for k, out in enumerate(outs):
        out[...] = upstream[k * tok : (k + 1) * tok, aligned(where[2] * half, half)]


def owner_kernel(n_dp, n_pipe, where, *refs):
    terms, ups, own, outs = refs[:n_pipe], refs[n_pipe : n_pipe + n_dp - 1], refs[-n_dp], refs[1 - n_dp :]
    tok, units = own.shape
    for k in range(n_dp):
        total_here = terms[0][k * tok : (k + 1) * tok, :]
        for term in terms[1:]:
            total_here = total_here + term[k * tok : (k + 1) * tok, :].astype(F32)
        if k == 0:
            own[...] = total_here
        else:
            outs[k - 1][:, :units] = total_here.astype(BF16)
            outs[k - 1][:, units:] = ups[k - 1][...]


def gate_and_up(packs, k, start, rows):
    pieces = [pack[aligned(start, rows), :] for pack in (packs[k], packs[len(packs) // 2 + k])]
    return jnp.concatenate(pieces, axis=1)


def forward_kernel(n_dp, where, *refs):
    packs, (x_mine, x_other, gain, resid, scale, pre, last, normed) = refs[: 2 * (n_dp - 1)], refs[2 * (n_dp - 1) :]
    ten = where[2]
    half = x_mine.shape[1]
    resid[:, aligned(ten * half, half)] = x_mine[...]
    resid[:, aligned((ten ^ 1) * half, half)] = x_other[...]
    values_in = resid[...].astype(F32)
    row_scale = lax.rsqrt(jnp.mean(values_in * values_in, axis=1, keepdims=True) + 1e-06)
    scale[...] = jnp.broadcast_to(row_scale, scale.shape)
    normed[...] = (values_in * row_scale * gain[...].astype(F32)).astype(BF16)
    cols = resid.shape[1] // n_dp
    result = jnp.zeros(pre.shape, F32)
    for k in range(n_dp - 1):
        left = normed[:, aligned((where[0] ^ k) * cols, cols)]
        result += jnp.dot(left, gate_and_up(packs, k, 0, cols), preferred_element_type=F32)
    last[...] = normed[:, aligned((where[0] ^ (n_dp - 1)) * cols, cols)]
    pre[...] = result


def terms_half(n_dp, n_pipe, n_ten, step, where, grads, pull, packs, scale, resid, gain, out, extra):
    pipe, ten = where[1], where[2]
    cols = resid.shape[1] // n_dp
    half = cols // n_ten
    share = half // n_pipe
    start = (ten ^ step) * half
    for k in range(n_dp):
        i = where[0] ^ k
        spot = aligned(i * cols + start, half)
        part = dot_nt(grads, gate_and_up(packs, k, start, half))
        part = scale * (gain[:, spot].astype(F32) * part) - resid[:, spot].astype(F32) * pull
        if extra is not None:
            part = part + extra[k][...].astype(F32)
        part = part.astype(out.dtype)
        for j in range(n_pipe):
            out[pipe ^ j, :, aligned(i * share, share)] = part[:, j * share : (j + 1) * share]


def backward_kernel(n_dp, n_pipe, n_ten, where, *refs):
    terms, packs = refs[:n_dp], refs[n_dp : 3 * n_dp]
    pre, last, scale, resid, gain, other, grads, pull = refs[3 * n_dp :]
    units = terms[0].shape[1]
    hidden_grad = terms[0][...]
    for term in terms[1:]:
        hidden_grad = hidden_grad + term[:, :units].astype(F32)
    both = gate_and_up(packs, n_dp - 1, 0, last.shape[1])
    pre_here = pre[...] + jnp.dot(last[...], both, preferred_element_type=F32)
    gate_pre, up_pre = pre_here[:, :units], pre_here[:, units:]
    gelu_value, gelu_slope = gelu_parts(gate_pre)
    gate_grad = hidden_grad * up_pre * gelu_slope
    up_grad = hidden_grad * gelu_value
    dotted = jnp.sum(gate_grad * gate_pre + up_grad * up_pre, axis=1, keepdims=True)
    grads[...] = jnp.concatenate([gate_grad, up_grad], axis=1).astype(BF16)
    row_scale = scale[:, :1]
    pull_here = row_scale * row_scale * (dotted / resid.shape[1])
    pull[...] = jnp.broadcast_to(pull_here, pull.shape)
    terms_half(
        n_dp, n_pipe, n_ten, 1, where, grads[...], pull_here, packs, row_scale, resid, gain, other, None
    )


def own_kernel(n_dp, n_pipe, n_ten, where, grads, pull, *refs):
    terms, upstream, packs = refs[: n_dp - 1], refs[n_dp - 1], refs[n_dp : 3 * n_dp]
    scale, resid, gain, mine = refs[3 * n_dp :]
    half = upstream.shape[1]
    extra = [upstream] + [term.at[:, term.shape[1] - half :] for term in terms]
    terms_half(
        n_dp, n_pipe, n_ten, 0, where, grads[...], pull[:, :1], packs, scale[:, :1], resid, gain, mine, extra
    )


def assemble_kernel(n_dp, n_pipe, n_ten, where, *refs):
    parts, (out, held, sems) = refs[:-3], refs[-3:]
    pipe, ten = where[1], where[2]
    share = parts[0].shape[1] // n_dp
    width = share * n_pipe
    copies = []
    for i in range(n_dp):
        for core in range(n_ten):
            at = i * n_ten + core
            for k in range(n_pipe):
                part = parts[core * n_pipe + k]
                held[at, :, aligned((pipe ^ k) * share, share)] = part[:, i * share : (i + 1) * share]
            spot = aligned((i * n_ten + (ten ^ core)) * width, width)
            copies.append(pltpu.make_async_copy(held.at[at], out.at[:, spot], sems.at[at]))
            copies[-1].start()
    for copy in copies:
        copy.wait()


def encoded_kernel(n_dp, n_ten, where, mine, other, own, near, far):
    dp, ten = where[0], where[2]
    tok, half = own.shape
    held = n_dp // n_ten
    for k, out in ((0, own), (1, near.at[:tok]), (3, near.at[tok:]), (2, far)):
        i = dp ^ k
        spot = aligned((lax.rem(i, held) * n_ten + ten) * half, half)
        here = i // held == ten

        @pl.when(here)
        def _(out=out, spot=spot):
            out[...] = mine[:, spot]

        @pl.when(jnp.logical_not(here))
        def _(out=out, spot=spot):
            out[...] = other[:, spot]


def kv_kernel(n_dp, where, *refs):
    pieces, (enc_mine, enc_other, out, grads) = refs[:n_dp], refs[n_dp:]
    tok = pieces[0].shape[0]
    half = enc_mine.shape[1]
    for k, piece in enumerate(pieces):
        grads[k * tok : (k + 1) * tok, :] = piece[...]
    for step, enc in ((0, enc_mine), (1, enc_other)):
        out[aligned((where[2] ^ step) * half, half), :] = lax.dot_general(
            enc[...], grads[...], (((0,), (0,)), ((), ())), preferred_element_type=F32
        ).astype(out.dtype)


def on_device(
    enc_out, mlp_input, grad_kv, kv_weight, gate_weight, up_weight, down_weight, norm_gain
):
    n_dp, n_pipe, n_ten = (lax.axis_size(a) for a in (DP, PIPE, TENSOR))
    tok = grad_kv.shape[0]
    width = norm_gain.shape[0]
    cols = kv_weight.shape[0]
    units = gate_weight.shape[1]
    share = cols // (n_pipe * n_ten)
    if (n_dp, n_pipe, n_ten) != (4, 4, 2) or share % 128 or tok % 128 or units % 128:
        return on_device_any(
            enc_out, mlp_input, grad_kv, kv_weight, gate_weight, up_weight, down_weight, norm_gain
        )
    where = jnp.stack([lax.axis_index(a) for a in (DP, PIPE, TENSOR)]).astype(jnp.int32)

    grads = gather(grad_kv.reshape(tok, -1), DP)
    x_other = send(mlp_input, TENSOR, 1)
    far, near = send(down_weight, PIPE, 2), send(down_weight, PIPE, 1)
    grads, gate, up = lax.optimization_barrier((grads, gate_weight, up_weight))
    near, first_gate, first_up = lax.optimization_barrier((near, gate_weight, up_weight))
    gates = [gate, send(first_gate, DP, 1), send(gate, DP, 2)]
    ups = [up, send(up, DP, 1), send(first_up, DP, 2)]
    grads, far, near = lax.optimization_barrier((grads, far, near))
    downs = [down_weight, near, far, send(far, PIPE, 1)]

    section = kv_weight.reshape(cols, -1)
    half = cols // n_ten
    (mine,) = call(
        lambda *refs: upstream_kernel(n_dp, *refs),
        "upstream_terms",
        [shaped((n_dp * tok, cols), BF16)],
        [where, *grads, section],
        [pltpu.VMEM((n_dp * tok, section.shape[1]), BF16)],
        flops=2 * n_dp * tok * section.size,
    )
    other = send(mine, TENSOR, 1)
    enc_other = send(enc_out, TENSOR, 1)
    other, x_other, enc_other = lax.optimization_barrier((other, x_other, enc_other))
    group = n_pipe * units
    outs = call(
        lambda *refs: hidden_kernel(n_dp, n_pipe, n_ten, *refs),
        "hidden_terms",
        [shaped((n_dp * tok, units), F32)]
        + [shaped((n_dp * tok, units), BF16)] * (n_pipe - 1)
        + [shaped((tok, half), BF16)] * n_dp,
        [where, mine, other, *downs],
        [pltpu.VMEM((n_dp * tok, cols), BF16), pltpu.VMEM((group, cols), BF16)],
        flops=2 * n_dp * tok * cols * group,
    )
    terms = [send(out, PIPE, k) for k, out in enumerate(outs[:n_pipe])]
    gain_row = norm_gain.reshape(1, width)
    resid, scale, pre, last = call(
        lambda *refs: forward_kernel(n_dp, *refs),
        "mlp_forward",
        [shaped((tok, width), BF16), shaped((tok, 128), F32), shaped((tok, 2 * units), F32), shaped((tok, cols), BF16)],
        [where, *gates, *ups, mlp_input, x_other, gain_row],
        [pltpu.VMEM((tok, width), BF16)],
        flops=4 * tok * width * units,
    )
    packs = [*gates, send(gates[1], DP, 2), *ups, send(ups[2], DP, 1)]
    terms, resid, scale, pre, last = lax.optimization_barrier((terms, resid, scale, pre, last))
    hidden, *sums = call(
        lambda *refs: owner_kernel(n_dp, n_pipe, *refs),
        "hidden_sums",
        [shaped((tok, units), F32)] + [shaped((tok, units + half), BF16)] * (n_dp - 1),
        [where, *terms, *outs[n_pipe + 1 :]],
    )
    terms = [hidden] + [send(part, DP, k) for k, part in enumerate(sums, 1)]
    encoded = [enc_out, enc_other]
    encoded = call(
        lambda *refs: encoded_kernel(n_dp, n_ten, *refs),
        "encoded_blocks",
        [shaped((tok, half), BF16), shaped((2 * tok, half), BF16), shaped((tok, half), BF16)],
        [where, *encoded],
    )
    terms, encoded = lax.optimization_barrier((terms, encoded))

    other, grads_both, pull = call(
        lambda *refs: backward_kernel(n_dp, n_pipe, n_ten, *refs),
        "mlp_backward",
        [shaped((n_pipe, tok, n_dp * share), BF16), shaped((tok, 2 * units), BF16), shaped((tok, 128), F32)],
        [where, *terms, *packs, pre, last, scale, resid, gain_row],
        flops=2 * tok * width * units,
    )
    (mine,) = call(
        lambda *refs: own_kernel(n_dp, n_pipe, n_ten, *refs),
        "own_terms",
        [shaped((n_pipe, tok, n_dp * share), F32)],
        [where, grads_both, pull, *terms[1:], outs[n_pipe], *packs, scale, resid, gain_row],
        flops=2 * tok * width * units,
    )
    mine = mine + send(other, TENSOR, 1).astype(F32)
    first = send(encoded[1], DP, 1)
    second = jnp.concatenate([encoded[2], first[tok:]], axis=0)
    mine, second = lax.optimization_barrier((mine, second))
    terms = [send(mine[k].astype(BF16), PIPE, k) for k in range(1, n_pipe)]
    second = send(second, DP, 2)
    part = mine[0]
    for term in terms:
        part = part + term.astype(F32)
    part = part.astype(BF16)
    part, second = lax.optimization_barrier((part, second))
    parts = gather(part, PIPE)

    mine_enc = jnp.concatenate([encoded[0], first[:tok], second], axis=0)
    (kv_grad,) = call(
        lambda *refs: kv_kernel(n_dp, *refs),
        "kv_grad",
        [shaped((cols, section.shape[1]), BF16)],
        [where, *grads, mine_enc, send(mine_enc, TENSOR, 1)],
        [pltpu.VMEM((n_dp * tok, section.shape[1]), BF16)],
        flops=2 * n_dp * tok * section.size,
    )
    kv_grad = kv_grad.reshape(kv_weight.shape)
    swapped = send(part, TENSOR, 1)
    parts, swapped, kv_grad = lax.optimization_barrier((parts, swapped, kv_grad))
    parts = parts + [swapped] + [send(part, TENSOR, 1) for part in parts[1:]]
    (input_grad,) = call(
        lambda *refs: assemble_kernel(n_dp, n_pipe, n_ten, *refs),
        "input_grad",
        [shaped((tok, width), BF16)],
        [where, *parts],
        [
            pltpu.VMEM((n_dp * n_ten, tok, width // (n_dp * n_ten)), BF16),
            pltpu.SemaphoreType.DMA((n_dp * n_ten,)),
        ],
        space=pl.ANY,
    )
    return (input_grad, kv_grad)


def solution(mesh):
    placed = (
        P(DP, TENSOR),
        P(DP, TENSOR),
        P(DP, None, PIPE, TENSOR),
        P(DP, None, PIPE, TENSOR),
        P(DP, (PIPE, TENSOR)),
        P(DP, (PIPE, TENSOR)),
        P((PIPE, TENSOR), DP),
        P(),
    )
    return jax.shard_map(
        on_device,
        mesh=mesh,
        in_specs=placed,
        out_specs=(P(DP, None), P(DP, None, PIPE, TENSOR)),
        check_vma=False,
    )
```

```python
import math

import jax
import jax.numpy as jnp
from jax import lax
from jax.experimental import pallas as pl
from jax.experimental.pallas import tpu as pltpu
from jax.sharding import PartitionSpec as P

DP, PIPE, TENSOR = "dp", "pipe", "tensor"
BF16, F32 = jnp.bfloat16, jnp.float32


def gelu_parts(preact):
    factor = math.sqrt(2.0 / math.pi)
    tangent = jnp.tanh(factor * (preact + 0.044715 * preact * preact * preact))
    gelu_value = 0.5 * preact * (1.0 + tangent)
    gelu_slope = 0.5 * (1.0 + tangent) + 0.5 * preact * (1.0 - tangent * tangent) * factor * (
        1.0 + 3.0 * 0.044715 * preact * preact
    )
    return (gelu_value, gelu_slope)


def send(value, axis, step):
    if step == 0:
        return value
    size = lax.axis_size(axis)
    return lax.ppermute(value, axis, [(src, src ^ step) for src in range(size)])


def gather(value, axis):
    return [send(value, axis, step) for step in range(lax.axis_size(axis))]


def natural(parts, axis, dim):
    mine = lax.axis_index(axis)
    width = parts[0].shape[dim]
    shape = list(parts[0].shape)
    shape[dim] = width * len(parts)
    out = jnp.zeros(shape, parts[0].dtype)
    for step, part in enumerate(parts):
        out = lax.dynamic_update_slice_in_dim(out, part, (mine ^ step) * width, dim)
    return out


def block(value, axis, step, dim):
    width = value.shape[dim] // lax.axis_size(axis)
    start = (lax.axis_index(axis) ^ step) * width
    return lax.dynamic_slice_in_dim(value, start, width, dim)


def total(blocks, axis):
    out = blocks[0].astype(F32)
    for step in range(1, len(blocks)):
        out = out + send(blocks[step].astype(BF16), axis, step).astype(F32)
    return out


def dot_nt(left, right):
    return lax.dot_general(left, right, (((1,), (1,)), ((), ())), preferred_element_type=F32)


def on_device_any(
    enc_out, mlp_input, grad_kv, kv_weight, gate_weight, up_weight, down_weight, norm_gain
):
    n_dp, n_pipe, n_ten = (lax.axis_size(a) for a in (DP, PIPE, TENSOR))
    tok = grad_kv.shape[0]
    width = norm_gain.shape[0]
    cols = kv_weight.shape[0]
    units = gate_weight.shape[1]
    share = cols // (n_pipe * n_ten)

    grads = jnp.concatenate(gather(grad_kv.reshape(tok, -1), DP), axis=0)

    section = kv_weight.reshape(cols, -1)
    partial = dot_nt(grads, section)
    partial = total([block(partial, TENSOR, k, 1) for k in range(n_ten)], TENSOR)
    partial = total([block(partial, PIPE, k, 1) for k in range(n_pipe)], PIPE)
    partial = partial.astype(BF16).reshape(n_dp, tok, share)
    upstream = jnp.concatenate([send(partial[k], DP, k) for k in range(n_dp)], axis=1)

    down = jnp.concatenate([send(block(down_weight, TENSOR, k, 1), TENSOR, k) for k in range(n_ten)], axis=0)
    down = jnp.concatenate([send(block(down, PIPE, k, 1), PIPE, k) for k in range(n_pipe)], axis=0)
    down = jnp.concatenate(gather(down, DP), axis=1)
    hidden = dot_nt(upstream, down).reshape(tok, n_pipe, n_ten, units)
    hidden = total([hidden[:, :, k] for k in range(n_ten)], TENSOR)
    hidden_grad = total([hidden[:, k] for k in range(n_pipe)], PIPE)

    both = jnp.concatenate([gate_weight, up_weight], axis=1)
    both = jnp.concatenate(gather(both, DP), axis=0)
    resid = natural(gather(mlp_input, TENSOR), TENSOR, 1)
    resid = jnp.concatenate([block(resid, DP, k, 1) for k in range(n_dp)], axis=1)
    gain_row = jnp.concatenate([block(norm_gain, DP, k, 0) for k in range(n_dp)], axis=0).astype(F32)
    values_in = resid.astype(F32)
    row_scale = lax.rsqrt(jnp.mean(values_in * values_in, axis=1, keepdims=True) + 1e-06)
    normed = (values_in * row_scale * gain_row).astype(BF16)
    pre = jnp.dot(normed, both, preferred_element_type=F32)
    gate_pre, up_pre = pre[:, :units], pre[:, units:]

    gelu_value, gelu_slope = gelu_parts(gate_pre)
    gate_grad = hidden_grad * up_pre * gelu_slope
    up_grad = hidden_grad * gelu_value
    dotted = jnp.sum(gate_grad * gate_pre + up_grad * up_pre, axis=1, keepdims=True)
    grads_both = jnp.concatenate([gate_grad, up_grad], axis=1).astype(BF16)
    normed_part = dot_nt(grads_both, both)
    part = row_scale * gain_row * normed_part - values_in * (row_scale * row_scale * (dotted / width))

    part = part.reshape(tok, n_dp, cols)
    part = total([block(part, TENSOR, k, 2) for k in range(n_ten)], TENSOR)
    part = total([block(part, PIPE, k, 2) for k in range(n_pipe)], PIPE)
    part = (part + upstream.reshape(tok, n_dp, share).astype(F32)).astype(BF16)
    whole = natural(gather(part, PIPE), PIPE, 2)
    whole = natural(gather(whole, TENSOR), TENSOR, 2)
    input_grad = natural([whole[:, k] for k in range(n_dp)], DP, 1)

    encoded = natural(gather(enc_out, TENSOR), TENSOR, 1)
    mine = [send(block(block(encoded, DP, k, 1), TENSOR, 0, 1), DP, k) for k in range(n_dp)]
    mine = jnp.concatenate(mine, axis=0)
    mine = natural(gather(mine, TENSOR), TENSOR, 1)
    kv_grad = lax.dot_general(
        mine, grads, (((0,), (0,)), ((), ())), preferred_element_type=F32
    ).astype(BF16)
    return (input_grad, kv_grad.reshape(kv_weight.shape))


def aligned(start, lanes):
    return pl.ds(pl.multiple_of(start, lanes), lanes)


def call(body, name, out, operands, scratch=(), flops=0, space=pltpu.VMEM):
    specs = [pl.BlockSpec(memory_space=pltpu.SMEM)]
    specs += [pl.BlockSpec(memory_space=pltpu.VMEM)] * (len(operands) - 1)
    moved = sum(a.size * a.dtype.itemsize for a in (*operands, *out))
    return pl.pallas_call(
        body,
        name=name,
        out_shape=out,
        in_specs=specs,
        out_specs=[pl.BlockSpec(memory_space=space)] * len(out),
        scratch_shapes=list(scratch),
        compiler_params=pltpu.CompilerParams(vmem_limit_bytes=40 * 1024 * 1024),
        cost_estimate=pl.CostEstimate(flops=flops, bytes_accessed=moved, transcendentals=0),
    )(*operands)


def shaped(shape, dtype):
    return jax.ShapeDtypeStruct(shape, dtype)


def upstream_kernel(n_dp, where, *refs):
    pieces, (section, out, grads) = refs[:n_dp], refs[n_dp:]
    tok = pieces[0].shape[0]
    for k, piece in enumerate(pieces):
        grads[k * tok : (k + 1) * tok, :] = piece[...]
    out[...] = dot_nt(grads[...], section[...]).astype(out.dtype)


def hidden_kernel(n_dp, n_pipe, n_ten, where, mine, other, *refs):
    downs, hidden, outs = refs[:n_pipe], refs[n_pipe : 2 * n_pipe], refs[2 * n_pipe : 2 * n_pipe + n_dp]
    upstream, down = refs[-2:]
    upstream[...] = (mine[...].astype(F32) + other[...].astype(F32)).astype(BF16)
    units = downs[0].shape[0]
    for k, part in enumerate(downs):
        down[k * units : (k + 1) * units, :] = part[...]
    result = dot_nt(upstream[...], down[...])
    for k, out in enumerate(hidden):
        out[...] = result[:, k * units : (k + 1) * units].astype(out.dtype)
    tok, half = outs[0].shape
    for k, out in enumerate(outs):
        out[...] = upstream[k * tok : (k + 1) * tok, aligned(where[2] * half, half)]


def owner_kernel(n_dp, n_pipe, where, *refs):
    terms, ups, own, outs = refs[:n_pipe], refs[n_pipe : n_pipe + n_dp - 1], refs[-n_dp], refs[1 - n_dp :]
    tok, units = own.shape
    for k in range(n_dp):
        total_here = terms[0][k * tok : (k + 1) * tok, :]
        for term in terms[1:]:
            total_here = total_here + term[k * tok : (k + 1) * tok, :].astype(F32)
        if k == 0:
            own[...] = total_here
        else:
            outs[k - 1][:, :units] = total_here.astype(BF16)
            outs[k - 1][:, units:] = ups[k - 1][...]


def gate_and_up(packs, k, start, rows):
    pieces = [pack[aligned(start, rows), :] for pack in (packs[k], packs[len(packs) // 2 + k])]
    return jnp.concatenate(pieces, axis=1)


def forward_kernel(n_dp, where, *refs):
    packs, (x_mine, x_other, gain, resid, scale, pre, last, normed) = refs[: 2 * (n_dp - 1)], refs[2 * (n_dp - 1) :]
    ten = where[2]
    half = x_mine.shape[1]
    resid[:, aligned(ten * half, half)] = x_mine[...]
    resid[:, aligned((ten ^ 1) * half, half)] = x_other[...]
    values_in = resid[...].astype(F32)
    row_scale = lax.rsqrt(jnp.mean(values_in * values_in, axis=1, keepdims=True) + 1e-06)
    scale[...] = jnp.broadcast_to(row_scale, scale.shape)
    normed[...] = (values_in * row_scale * gain[...].astype(F32)).astype(BF16)
    cols = resid.shape[1] // n_dp
    result = jnp.zeros(pre.shape, F32)
    for k in range(n_dp - 1):
        left = normed[:, aligned((where[0] ^ k) * cols, cols)]
        result += jnp.dot(left, gate_and_up(packs, k, 0, cols), preferred_element_type=F32)
    last[...] = normed[:, aligned((where[0] ^ (n_dp - 1)) * cols, cols)]
    pre[...] = result


def terms_half(n_dp, n_pipe, n_ten, step, where, grads, pull, packs, scale, resid, gain, out, extra):
    pipe, ten = where[1], where[2]
    cols = resid.shape[1] // n_dp
    half = cols // n_ten
    share = half // n_pipe
    start = (ten ^ step) * half
    for k in range(n_dp):
        i = where[0] ^ k
        spot = aligned(i * cols + start, half)
        part = dot_nt(grads, gate_and_up(packs, k, start, half))
        part = scale * (gain[:, spot].astype(F32) * part) - resid[:, spot].astype(F32) * pull
        if extra is not None:
            part = part + extra[k][...].astype(F32)
        part = part.astype(out.dtype)
        for j in range(n_pipe):
            out[pipe ^ j, :, aligned(i * share, share)] = part[:, j * share : (j + 1) * share]


def backward_kernel(n_dp, n_pipe, n_ten, where, *refs):
    terms, packs = refs[:n_dp], refs[n_dp : 3 * n_dp]
    pre, last, scale, resid, gain, other, grads, pull = refs[3 * n_dp :]
    units = terms[0].shape[1]
    hidden_grad = terms[0][...]
    for term in terms[1:]:
        hidden_grad = hidden_grad + term[:, :units].astype(F32)
    both = gate_and_up(packs, n_dp - 1, 0, last.shape[1])
    pre_here = pre[...] + jnp.dot(last[...], both, preferred_element_type=F32)
    gate_pre, up_pre = pre_here[:, :units], pre_here[:, units:]
    gelu_value, gelu_slope = gelu_parts(gate_pre)
    gate_grad = hidden_grad * up_pre * gelu_slope
    up_grad = hidden_grad * gelu_value
    dotted = jnp.sum(gate_grad * gate_pre + up_grad * up_pre, axis=1, keepdims=True)
    grads[...] = jnp.concatenate([gate_grad, up_grad], axis=1).astype(BF16)
    row_scale = scale[:, :1]
    pull_here = row_scale * row_scale * (dotted / resid.shape[1])
    pull[...] = jnp.broadcast_to(pull_here, pull.shape)
    terms_half(
        n_dp, n_pipe, n_ten, 1, where, grads[...], pull_here, packs, row_scale, resid, gain, other, None
    )


def own_kernel(n_dp, n_pipe, n_ten, where, grads, pull, *refs):
    terms, upstream, packs = refs[: n_dp - 1], refs[n_dp - 1], refs[n_dp : 3 * n_dp]
    scale, resid, gain, mine = refs[3 * n_dp :]
    half = upstream.shape[1]
    extra = [upstream] + [term.at[:, term.shape[1] - half :] for term in terms]
    terms_half(
        n_dp, n_pipe, n_ten, 0, where, grads[...], pull[:, :1], packs, scale[:, :1], resid, gain, mine, extra
    )


def assemble_kernel(n_dp, n_pipe, n_ten, where, *refs):
    parts, (out, held, sems) = refs[:-3], refs[-3:]
    pipe, ten = where[1], where[2]
    share = parts[0].shape[1] // n_dp
    width = share * n_pipe
    copies = []
    for i in range(n_dp):
        for core in range(n_ten):
            at = i * n_ten + core
            for k in range(n_pipe):
                part = parts[core * n_pipe + k]
                held[at, :, aligned((pipe ^ k) * share, share)] = part[:, i * share : (i + 1) * share]
            spot = aligned((i * n_ten + (ten ^ core)) * width, width)
            copies.append(pltpu.make_async_copy(held.at[at], out.at[:, spot], sems.at[at]))
            copies[-1].start()
    for copy in copies:
        copy.wait()


def encoded_kernel(n_dp, n_ten, where, mine, other, own, near, far):
    dp, ten = where[0], where[2]
    tok, half = own.shape
    held = n_dp // n_ten
    for k, out in ((0, own), (1, near.at[:tok]), (3, near.at[tok:]), (2, far)):
        i = dp ^ k
        spot = aligned((lax.rem(i, held) * n_ten + ten) * half, half)
        here = i // held == ten

        @pl.when(here)
        def _(out=out, spot=spot):
            out[...] = mine[:, spot]

        @pl.when(jnp.logical_not(here))
        def _(out=out, spot=spot):
            out[...] = other[:, spot]


def kv_kernel(n_dp, where, *refs):
    pieces, (enc_mine, enc_other, out, grads) = refs[:n_dp], refs[n_dp:]
    tok = pieces[0].shape[0]
    half = enc_mine.shape[1]
    for k, piece in enumerate(pieces):
        grads[k * tok : (k + 1) * tok, :] = piece[...]
    for step, enc in ((0, enc_mine), (1, enc_other)):
        out[aligned((where[2] ^ step) * half, half), :] = lax.dot_general(
            enc[...], grads[...], (((0,), (0,)), ((), ())), preferred_element_type=F32
        ).astype(out.dtype)


def on_device(
    enc_out, mlp_input, grad_kv, kv_weight, gate_weight, up_weight, down_weight, norm_gain
):
    n_dp, n_pipe, n_ten = (lax.axis_size(a) for a in (DP, PIPE, TENSOR))
    tok = grad_kv.shape[0]
    width = norm_gain.shape[0]
    cols = kv_weight.shape[0]
    units = gate_weight.shape[1]
    share = cols // (n_pipe * n_ten)
    squares = n_dp == n_pipe == n_ten * n_ten and n_ten == 2
    if not squares or share % 128 or tok % 128 or units % 128:
        return on_device_any(
            enc_out, mlp_input, grad_kv, kv_weight, gate_weight, up_weight, down_weight, norm_gain
        )
    where = jnp.stack([lax.axis_index(a) for a in (DP, PIPE, TENSOR)]).astype(jnp.int32)

    grads = gather(grad_kv.reshape(tok, -1), DP)
    x_other = send(mlp_input, TENSOR, 1)
    far, near = send(down_weight, PIPE, 2), send(down_weight, PIPE, 1)
    grads, gate, up = lax.optimization_barrier((grads, gate_weight, up_weight))
    near, first_gate, first_up = lax.optimization_barrier((near, gate_weight, up_weight))
    gates = [gate, send(first_gate, DP, 1), send(gate, DP, 2)]
    ups = [up, send(up, DP, 1), send(first_up, DP, 2)]
    grads, far, near = lax.optimization_barrier((grads, far, near))
    downs = [down_weight, near, far, send(far, PIPE, 1)]

    section = kv_weight.reshape(cols, -1)
    half = cols // n_ten
    (mine,) = call(
        lambda *refs: upstream_kernel(n_dp, *refs),
        "upstream_terms",
        [shaped((n_dp * tok, cols), BF16)],
        [where, *grads, section],
        [pltpu.VMEM((n_dp * tok, section.shape[1]), BF16)],
        flops=2 * n_dp * tok * section.size,
    )
    other = send(mine, TENSOR, 1)
    enc_other = send(enc_out, TENSOR, 1)
    other, x_other, enc_other = lax.optimization_barrier((other, x_other, enc_other))
    group = n_pipe * units
    outs = call(
        lambda *refs: hidden_kernel(n_dp, n_pipe, n_ten, *refs),
        "hidden_terms",
        [shaped((n_dp * tok, units), F32)]
        + [shaped((n_dp * tok, units), BF16)] * (n_pipe - 1)
        + [shaped((tok, half), BF16)] * n_dp,
        [where, mine, other, *downs],
        [pltpu.VMEM((n_dp * tok, cols), BF16), pltpu.VMEM((group, cols), BF16)],
        flops=2 * n_dp * tok * cols * group,
    )
    terms = [send(out, PIPE, k) for k, out in enumerate(outs[:n_pipe])]
    gain_row = norm_gain.reshape(1, width)
    resid, scale, pre, last = call(
        lambda *refs: forward_kernel(n_dp, *refs),
        "mlp_forward",
        [shaped((tok, width), BF16), shaped((tok, 128), F32), shaped((tok, 2 * units), F32), shaped((tok, cols), BF16)],
        [where, *gates, *ups, mlp_input, x_other, gain_row],
        [pltpu.VMEM((tok, width), BF16)],
        flops=4 * tok * width * units,
    )
    packs = [*gates, send(gates[1], DP, 2), *ups, send(ups[2], DP, 1)]
    terms, resid, scale, pre, last = lax.optimization_barrier((terms, resid, scale, pre, last))
    hidden, *sums = call(
        lambda *refs: owner_kernel(n_dp, n_pipe, *refs),
        "hidden_sums",
        [shaped((tok, units), F32)] + [shaped((tok, units + half), BF16)] * (n_dp - 1),
        [where, *terms, *outs[n_pipe + 1 :]],
    )
    terms = [hidden] + [send(part, DP, k) for k, part in enumerate(sums, 1)]
    encoded = [enc_out, enc_other]
    encoded = call(
        lambda *refs: encoded_kernel(n_dp, n_ten, *refs),
        "encoded_blocks",
        [shaped((tok, half), BF16), shaped((2 * tok, half), BF16), shaped((tok, half), BF16)],
        [where, *encoded],
    )
    terms, encoded = lax.optimization_barrier((terms, encoded))

    other, grads_both, pull = call(
        lambda *refs: backward_kernel(n_dp, n_pipe, n_ten, *refs),
        "mlp_backward",
        [shaped((n_pipe, tok, n_dp * share), BF16), shaped((tok, 2 * units), BF16), shaped((tok, 128), F32)],
        [where, *terms, *packs, pre, last, scale, resid, gain_row],
        flops=2 * tok * width * units,
    )
    (mine,) = call(
        lambda *refs: own_kernel(n_dp, n_pipe, n_ten, *refs),
        "own_terms",
        [shaped((n_pipe, tok, n_dp * share), F32)],
        [where, grads_both, pull, *terms[1:], outs[n_pipe], *packs, scale, resid, gain_row],
        flops=2 * tok * width * units,
    )
    mine = mine + send(other, TENSOR, 1).astype(F32)
    first = send(encoded[1], DP, 1)
    second = jnp.concatenate([encoded[2], first[tok:]], axis=0)
    mine, second = lax.optimization_barrier((mine, second))
    terms = [send(mine[k].astype(BF16), PIPE, k) for k in range(1, n_pipe)]
    second = send(second, DP, 2)
    part = mine[0]
    for term in terms:
        part = part + term.astype(F32)
    part = part.astype(BF16)
    part, second = lax.optimization_barrier((part, second))
    parts = gather(part, PIPE)

    mine_enc = jnp.concatenate([encoded[0], first[:tok], second], axis=0)
    (kv_grad,) = call(
        lambda *refs: kv_kernel(n_dp, *refs),
        "kv_grad",
        [shaped((cols, section.shape[1]), BF16)],
        [where, *grads, mine_enc, send(mine_enc, TENSOR, 1)],
        [pltpu.VMEM((n_dp * tok, section.shape[1]), BF16)],
        flops=2 * n_dp * tok * section.size,
    )
    kv_grad = kv_grad.reshape(kv_weight.shape)
    swapped = [send(part, TENSOR, 1) for part in parts[:2]]
    far, last, kv_grad = lax.optimization_barrier((*parts[2:], kv_grad))
    parts = [*parts[:2], far, last, *swapped, send(far, TENSOR, 1), send(last, TENSOR, 1)]
    (input_grad,) = call(
        lambda *refs: assemble_kernel(n_dp, n_pipe, n_ten, *refs),
        "input_grad",
        [shaped((tok, width), BF16)],
        [where, *parts],
        [
            pltpu.VMEM((n_dp * n_ten, tok, width // (n_dp * n_ten)), BF16),
            pltpu.SemaphoreType.DMA((n_dp * n_ten,)),
        ],
        space=pl.ANY,
    )
    return (input_grad, kv_grad)


def solution(mesh):
    placed = (
        P(DP, TENSOR),
        P(DP, TENSOR),
        P(DP, None, PIPE, TENSOR),
        P(DP, None, PIPE, TENSOR),
        P(DP, (PIPE, TENSOR)),
        P(DP, (PIPE, TENSOR)),
        P((PIPE, TENSOR), DP),
        P(),
    )
    return jax.shard_map(
        on_device,
        mesh=mesh,
        in_specs=placed,
        out_specs=(P(DP, None), P(DP, None, PIPE, TENSOR)),
        check_vma=False,
    )
```

```python
import math

import jax
import jax.numpy as jnp
from jax import lax
from jax.experimental import pallas as pl
from jax.experimental.pallas import tpu as pltpu
from jax.sharding import PartitionSpec as P

DP, PIPE, TENSOR = "dp", "pipe", "tensor"
BF16, F32 = jnp.bfloat16, jnp.float32


def gelu_parts(preact):
    factor = math.sqrt(2.0 / math.pi)
    tangent = jnp.tanh(factor * (preact + 0.044715 * preact * preact * preact))
    gelu_value = 0.5 * preact * (1.0 + tangent)
    gelu_slope = 0.5 * (1.0 + tangent) + 0.5 * preact * (1.0 - tangent * tangent) * factor * (
        1.0 + 3.0 * 0.044715 * preact * preact
    )
    return (gelu_value, gelu_slope)


def send(value, axis, step):
    if step == 0:
        return value
    size = lax.axis_size(axis)
    return lax.ppermute(value, axis, [(src, src ^ step) for src in range(size)])


def gather(value, axis):
    return [send(value, axis, step) for step in range(lax.axis_size(axis))]


def natural(parts, axis, dim):
    mine = lax.axis_index(axis)
    width = parts[0].shape[dim]
    shape = list(parts[0].shape)
    shape[dim] = width * len(parts)
    out = jnp.zeros(shape, parts[0].dtype)
    for step, part in enumerate(parts):
        out = lax.dynamic_update_slice_in_dim(out, part, (mine ^ step) * width, dim)
    return out


def block(value, axis, step, dim):
    width = value.shape[dim] // lax.axis_size(axis)
    start = (lax.axis_index(axis) ^ step) * width
    return lax.dynamic_slice_in_dim(value, start, width, dim)


def total(blocks, axis):
    out = blocks[0].astype(F32)
    for step in range(1, len(blocks)):
        out = out + send(blocks[step].astype(BF16), axis, step).astype(F32)
    return out


def dot_nt(left, right):
    return lax.dot_general(left, right, (((1,), (1,)), ((), ())), preferred_element_type=F32)


def on_device_any(
    enc_out, mlp_input, grad_kv, kv_weight, gate_weight, up_weight, down_weight, norm_gain
):
    n_dp, n_pipe, n_ten = (lax.axis_size(a) for a in (DP, PIPE, TENSOR))
    tok = grad_kv.shape[0]
    width = norm_gain.shape[0]
    cols = kv_weight.shape[0]
    units = gate_weight.shape[1]
    share = cols // (n_pipe * n_ten)

    grads = jnp.concatenate(gather(grad_kv.reshape(tok, -1), DP), axis=0)

    section = kv_weight.reshape(cols, -1)
    partial = dot_nt(grads, section)
    partial = total([block(partial, TENSOR, k, 1) for k in range(n_ten)], TENSOR)
    partial = total([block(partial, PIPE, k, 1) for k in range(n_pipe)], PIPE)
    partial = partial.astype(BF16).reshape(n_dp, tok, share)
    upstream = jnp.concatenate([send(partial[k], DP, k) for k in range(n_dp)], axis=1)

    down = jnp.concatenate([send(block(down_weight, TENSOR, k, 1), TENSOR, k) for k in range(n_ten)], axis=0)
    down = jnp.concatenate([send(block(down, PIPE, k, 1), PIPE, k) for k in range(n_pipe)], axis=0)
    down = jnp.concatenate(gather(down, DP), axis=1)
    hidden = dot_nt(upstream, down).reshape(tok, n_pipe, n_ten, units)
    hidden = total([hidden[:, :, k] for k in range(n_ten)], TENSOR)
    hidden_grad = total([hidden[:, k] for k in range(n_pipe)], PIPE)

    both = jnp.concatenate([gate_weight, up_weight], axis=1)
    both = jnp.concatenate(gather(both, DP), axis=0)
    resid = natural(gather(mlp_input, TENSOR), TENSOR, 1)
    resid = jnp.concatenate([block(resid, DP, k, 1) for k in range(n_dp)], axis=1)
    gain_row = jnp.concatenate([block(norm_gain, DP, k, 0) for k in range(n_dp)], axis=0).astype(F32)
    values_in = resid.astype(F32)
    row_scale = lax.rsqrt(jnp.mean(values_in * values_in, axis=1, keepdims=True) + 1e-06)
    normed = (values_in * row_scale * gain_row).astype(BF16)
    pre = jnp.dot(normed, both, preferred_element_type=F32)
    gate_pre, up_pre = pre[:, :units], pre[:, units:]

    gelu_value, gelu_slope = gelu_parts(gate_pre)
    gate_grad = hidden_grad * up_pre * gelu_slope
    up_grad = hidden_grad * gelu_value
    dotted = jnp.sum(gate_grad * gate_pre + up_grad * up_pre, axis=1, keepdims=True)
    grads_both = jnp.concatenate([gate_grad, up_grad], axis=1).astype(BF16)
    normed_part = dot_nt(grads_both, both)
    part = row_scale * gain_row * normed_part - values_in * (row_scale * row_scale * (dotted / width))

    part = part.reshape(tok, n_dp, cols)
    part = total([block(part, TENSOR, k, 2) for k in range(n_ten)], TENSOR)
    part = total([block(part, PIPE, k, 2) for k in range(n_pipe)], PIPE)
    part = (part + upstream.reshape(tok, n_dp, share).astype(F32)).astype(BF16)
    whole = natural(gather(part, PIPE), PIPE, 2)
    whole = natural(gather(whole, TENSOR), TENSOR, 2)
    input_grad = natural([whole[:, k] for k in range(n_dp)], DP, 1)

    encoded = natural(gather(enc_out, TENSOR), TENSOR, 1)
    mine = [send(block(block(encoded, DP, k, 1), TENSOR, 0, 1), DP, k) for k in range(n_dp)]
    mine = jnp.concatenate(mine, axis=0)
    mine = natural(gather(mine, TENSOR), TENSOR, 1)
    kv_grad = lax.dot_general(
        mine, grads, (((0,), (0,)), ((), ())), preferred_element_type=F32
    ).astype(BF16)
    return (input_grad, kv_grad.reshape(kv_weight.shape))


def aligned(start, lanes):
    return pl.ds(pl.multiple_of(start, lanes), lanes)


def call(body, name, out, operands, scratch=(), flops=0, space=pltpu.VMEM):
    specs = [pl.BlockSpec(memory_space=pltpu.SMEM)]
    specs += [pl.BlockSpec(memory_space=pltpu.VMEM)] * (len(operands) - 1)
    moved = sum(a.size * a.dtype.itemsize for a in (*operands, *out))
    return pl.pallas_call(
        body,
        name=name,
        out_shape=out,
        in_specs=specs,
        out_specs=[pl.BlockSpec(memory_space=space)] * len(out),
        scratch_shapes=list(scratch),
        compiler_params=pltpu.CompilerParams(vmem_limit_bytes=40 * 1024 * 1024),
        cost_estimate=pl.CostEstimate(flops=flops, bytes_accessed=moved, transcendentals=0),
    )(*operands)


def shaped(shape, dtype):
    return jax.ShapeDtypeStruct(shape, dtype)


def upstream_kernel(n_dp, where, *refs):
    pieces, (section, out, grads) = refs[:n_dp], refs[n_dp:]
    tok = pieces[0].shape[0]
    for k, piece in enumerate(pieces):
        grads[k * tok : (k + 1) * tok, :] = piece[...]
    out[...] = dot_nt(grads[...], section[...]).astype(out.dtype)


def hidden_kernel(n_parts, n_ten, where, mine, other, *refs):
    downs, hidden, outs = refs[:n_parts], refs[n_parts : 2 * n_parts], refs[2 * n_parts : -2]
    upstream, down = refs[-2:]
    upstream[...] = (mine[...].astype(F32) + other[...].astype(F32)).astype(BF16)
    units = downs[0].shape[0]
    for k, part in enumerate(downs):
        down[k * units : (k + 1) * units, :] = part[...]
    result = dot_nt(upstream[...], down[...])
    for k, out in enumerate(hidden):
        out[...] = result[:, k * units : (k + 1) * units].astype(out.dtype)
    for k, out in enumerate(outs):
        tok, half = out.shape
        out[...] = upstream[k * tok : (k + 1) * tok, aligned(where[2] * half, half)]


def owner_kernel(n_dp, n_pipe, where, *refs):
    terms, ups, own, outs = refs[:n_pipe], refs[n_pipe : n_pipe + n_dp - 1], refs[-n_dp], refs[1 - n_dp :]
    tok, units = own.shape
    for k in range(n_dp):
        total_here = terms[0][k * tok : (k + 1) * tok, :]
        for term in terms[1:]:
            total_here = total_here + term[k * tok : (k + 1) * tok, :].astype(F32)
        if k == 0:
            own[...] = total_here
        else:
            outs[k - 1][:, :units] = total_here.astype(BF16)
            outs[k - 1][:, units:] = ups[k - 1][...]


def gate_and_up(packs, k, start, rows):
    pieces = [pack[aligned(start, rows), :] for pack in (packs[k], packs[len(packs) // 2 + k])]
    return jnp.concatenate(pieces, axis=1)


def forward_kernel(n_dp, where, *refs):
    packs, (x_mine, x_other, gain, resid, scale, pre, last, normed) = refs[: 2 * (n_dp - 1)], refs[2 * (n_dp - 1) :]
    ten = where[2]
    half = x_mine.shape[1]
    resid[:, aligned(ten * half, half)] = x_mine[...]
    resid[:, aligned((ten ^ 1) * half, half)] = x_other[...]
    values_in = resid[...].astype(F32)
    row_scale = lax.rsqrt(jnp.mean(values_in * values_in, axis=1, keepdims=True) + 1e-06)
    scale[...] = jnp.broadcast_to(row_scale, scale.shape)
    normed[...] = (values_in * row_scale * gain[...].astype(F32)).astype(BF16)
    cols = resid.shape[1] // n_dp
    result = jnp.zeros(pre.shape, F32)
    for k in range(n_dp - 1):
        left = normed[:, aligned((where[0] ^ k) * cols, cols)]
        result += jnp.dot(left, gate_and_up(packs, k, 0, cols), preferred_element_type=F32)
    last[...] = normed[:, aligned((where[0] ^ (n_dp - 1)) * cols, cols)]
    pre[...] = result


def terms_half(n_dp, n_pipe, n_ten, step, where, grads, pull, packs, scale, resid, gain, out, extra):
    pipe, ten = where[1], where[2]
    cols = resid.shape[1] // n_dp
    half = cols // n_ten
    share = half // n_pipe
    start = (ten ^ step) * half
    for k in range(n_dp):
        i = where[0] ^ k
        spot = aligned(i * cols + start, half)
        part = dot_nt(grads, gate_and_up(packs, k, start, half))
        part = scale * (gain[:, spot].astype(F32) * part) - resid[:, spot].astype(F32) * pull
        if extra is not None:
            part = part + extra[k][...].astype(F32)
        part = part.astype(out.dtype)
        for j in range(n_pipe):
            out[pipe ^ j, :, aligned(i * share, share)] = part[:, j * share : (j + 1) * share]


def backward_kernel(n_dp, n_pipe, n_ten, where, *refs):
    terms, packs = refs[:n_dp], refs[n_dp : 3 * n_dp]
    pre, last, scale, resid, gain, other, grads, pull = refs[3 * n_dp :]
    units = terms[0].shape[1]
    hidden_grad = terms[0][...]
    for term in terms[1:]:
        hidden_grad = hidden_grad + term[:, :units].astype(F32)
    both = gate_and_up(packs, n_dp - 1, 0, last.shape[1])
    pre_here = pre[...] + jnp.dot(last[...], both, preferred_element_type=F32)
    gate_pre, up_pre = pre_here[:, :units], pre_here[:, units:]
    gelu_value, gelu_slope = gelu_parts(gate_pre)
    gate_grad = hidden_grad * up_pre * gelu_slope
    up_grad = hidden_grad * gelu_value
    dotted = jnp.sum(gate_grad * gate_pre + up_grad * up_pre, axis=1, keepdims=True)
    grads[...] = jnp.concatenate([gate_grad, up_grad], axis=1).astype(BF16)
    row_scale = scale[:, :1]
    pull_here = row_scale * row_scale * (dotted / resid.shape[1])
    pull[...] = jnp.broadcast_to(pull_here, pull.shape)
    terms_half(
        n_dp, n_pipe, n_ten, 1, where, grads[...], pull_here, packs, row_scale, resid, gain, other, None
    )


def own_kernel(n_dp, n_pipe, n_ten, where, grads, pull, *refs):
    terms, upstream, packs = refs[: n_dp - 1], refs[n_dp - 1], refs[n_dp : 3 * n_dp]
    scale, resid, gain, mine = refs[3 * n_dp :]
    half = upstream.shape[1]
    extra = [upstream] + [term.at[:, term.shape[1] - half :] for term in terms]
    terms_half(
        n_dp, n_pipe, n_ten, 0, where, grads[...], pull[:, :1], packs, scale[:, :1], resid, gain, mine, extra
    )


def assemble_kernel(n_dp, n_pipe, n_ten, where, *refs):
    parts, (out, held, sems) = refs[:-3], refs[-3:]
    pipe, ten = where[1], where[2]
    share = parts[0].shape[1] // n_dp
    width = share * n_pipe
    copies = []
    for i in range(n_dp):
        for core in range(n_ten):
            at = i * n_ten + core
            for k in range(n_pipe):
                part = parts[core * n_pipe + k]
                held[at, :, aligned((pipe ^ k) * share, share)] = part[:, i * share : (i + 1) * share]
            spot = aligned((i * n_ten + (ten ^ core)) * width, width)
            copies.append(pltpu.make_async_copy(held.at[at], out.at[:, spot], sems.at[at]))
            copies[-1].start()
    for copy in copies:
        copy.wait()


def encoded_kernel(n_dp, n_ten, where, mine, other, own, near, far):
    dp, ten = where[0], where[2]
    tok, half = own.shape
    held = n_dp // n_ten
    for k, out in ((0, own), (1, near.at[:tok]), (3, near.at[tok:]), (2, far)):
        i = dp ^ k
        spot = aligned((lax.rem(i, held) * n_ten + ten) * half, half)
        here = i // held == ten

        @pl.when(here)
        def _(out=out, spot=spot):
            out[...] = mine[:, spot]

        @pl.when(jnp.logical_not(here))
        def _(out=out, spot=spot):
            out[...] = other[:, spot]


def kv_kernel(n_dp, where, *refs):
    pieces, (enc_mine, enc_other, out, grads) = refs[:n_dp], refs[n_dp:]
    tok = pieces[0].shape[0]
    half = enc_mine.shape[1]
    for k, piece in enumerate(pieces):
        grads[k * tok : (k + 1) * tok, :] = piece[...]
    for step, enc in ((0, enc_mine), (1, enc_other)):
        out[aligned((where[2] ^ step) * half, half), :] = lax.dot_general(
            enc[...], grads[...], (((0,), (0,)), ((), ())), preferred_element_type=F32
        ).astype(out.dtype)


def on_device(
    enc_out, mlp_input, grad_kv, kv_weight, gate_weight, up_weight, down_weight, norm_gain
):
    n_dp, n_pipe, n_ten = (lax.axis_size(a) for a in (DP, PIPE, TENSOR))
    tok = grad_kv.shape[0]
    width = norm_gain.shape[0]
    cols = kv_weight.shape[0]
    units = gate_weight.shape[1]
    share = cols // (n_pipe * n_ten)
    squares = n_dp == n_pipe == n_ten * n_ten and n_ten == 2
    if not squares or share % 128 or tok % 128 or units % 128:
        return on_device_any(
            enc_out, mlp_input, grad_kv, kv_weight, gate_weight, up_weight, down_weight, norm_gain
        )
    where = jnp.stack([lax.axis_index(a) for a in (DP, PIPE, TENSOR)]).astype(jnp.int32)

    grads = gather(grad_kv.reshape(tok, -1), DP)
    x_other = send(mlp_input, TENSOR, 1)
    far, near = send(down_weight, PIPE, 2), send(down_weight, PIPE, 1)
    grads, gate, up = lax.optimization_barrier((grads, gate_weight, up_weight))
    gates = [gate, send(gate, DP, 1), send(gate, DP, 2)]
    ups = [up, send(up, DP, 1), send(up, DP, 2)]
    grads, far, near = lax.optimization_barrier((grads, far, near))
    downs = [down_weight, near, far, send(far, PIPE, 1)]

    section = kv_weight.reshape(cols, -1)
    half = cols // n_ten
    (mine,) = call(
        lambda *refs: upstream_kernel(n_dp, *refs),
        "upstream_terms",
        [shaped((n_dp * tok, cols), BF16)],
        [where, *grads, section],
        [pltpu.VMEM((n_dp * tok, section.shape[1]), BF16)],
        flops=2 * n_dp * tok * section.size,
    )
    other = send(mine, TENSOR, 1)
    enc_other = send(enc_out, TENSOR, 1)
    other, x_other, enc_other = lax.optimization_barrier((other, x_other, enc_other))
    group = n_pipe * units
    outs = call(
        lambda *refs: hidden_kernel(n_pipe - 1, n_ten, *refs),
        "hidden_terms",
        [shaped((n_dp * tok, units), F32)]
        + [shaped((n_dp * tok, units), BF16)] * (n_pipe - 2)
        + [shaped((tok, half), BF16)] * n_dp,
        [where, mine, other, *downs[:-1]],
        [pltpu.VMEM((n_dp * tok, cols), BF16), pltpu.VMEM((group - units, cols), BF16)],
        flops=2 * n_dp * tok * cols * group,
    )
    (last_out,) = call(
        lambda *refs: hidden_kernel(1, n_ten, *refs),
        "hidden_last",
        [shaped((n_dp * tok, units), BF16)],
        [where, mine, other, downs[-1]],
        [pltpu.VMEM((n_dp * tok, cols), BF16), pltpu.VMEM((units, cols), BF16)],
        flops=2 * n_dp * tok * cols * units,
    )
    outs = [*outs[: n_pipe - 1], last_out, *outs[n_pipe - 1 :]]
    terms = [send(out, PIPE, k) for k, out in enumerate(outs[:n_pipe])]
    gain_row = norm_gain.reshape(1, width)
    resid, scale, pre, last = call(
        lambda *refs: forward_kernel(n_dp, *refs),
        "mlp_forward",
        [shaped((tok, width), BF16), shaped((tok, 128), F32), shaped((tok, 2 * units), F32), shaped((tok, cols), BF16)],
        [where, *gates, *ups, mlp_input, x_other, gain_row],
        [pltpu.VMEM((tok, width), BF16)],
        flops=4 * tok * width * units,
    )
    packs = [*gates, send(gates[1], DP, 2), *ups, send(ups[2], DP, 1)]
    terms, resid, scale, pre, last = lax.optimization_barrier((terms, resid, scale, pre, last))
    hidden, *sums = call(
        lambda *refs: owner_kernel(n_dp, n_pipe, *refs),
        "hidden_sums",
        [shaped((tok, units), F32)] + [shaped((tok, units + half), BF16)] * (n_dp - 1),
        [where, *terms, *outs[n_pipe + 1 :]],
    )
    terms = [hidden] + [send(part, DP, k) for k, part in enumerate(sums, 1)]
    encoded = [enc_out, enc_other]
    encoded = call(
        lambda *refs: encoded_kernel(n_dp, n_ten, *refs),
        "encoded_blocks",
        [shaped((tok, half), BF16), shaped((2 * tok, half), BF16), shaped((tok, half), BF16)],
        [where, *encoded],
    )
    terms, encoded = lax.optimization_barrier((terms, encoded))

    other, grads_both, pull = call(
        lambda *refs: backward_kernel(n_dp, n_pipe, n_ten, *refs),
        "mlp_backward",
        [shaped((n_pipe, tok, n_dp * share), BF16), shaped((tok, 2 * units), BF16), shaped((tok, 128), F32)],
        [where, *terms, *packs, pre, last, scale, resid, gain_row],
        flops=2 * tok * width * units,
    )
    (mine,) = call(
        lambda *refs: own_kernel(n_dp, n_pipe, n_ten, *refs),
        "own_terms",
        [shaped((n_pipe, tok, n_dp * share), F32)],
        [where, grads_both, pull, *terms[1:], outs[n_pipe], *packs, scale, resid, gain_row],
        flops=2 * tok * width * units,
    )
    mine = mine + send(other, TENSOR, 1).astype(F32)
    first = send(encoded[1], DP, 1)
    second = jnp.concatenate([encoded[2], first[tok:]], axis=0)
    mine, second = lax.optimization_barrier((mine, second))
    terms = [send(mine[k].astype(BF16), PIPE, k) for k in range(1, n_pipe)]
    second = send(second, DP, 2)
    part = mine[0]
    for term in terms:
        part = part + term.astype(F32)
    part = part.astype(BF16)
    part, second = lax.optimization_barrier((part, second))
    parts = gather(part, PIPE)

    mine_enc = jnp.concatenate([encoded[0], first[:tok], second], axis=0)
    (kv_grad,) = call(
        lambda *refs: kv_kernel(n_dp, *refs),
        "kv_grad",
        [shaped((cols, section.shape[1]), BF16)],
        [where, *grads, mine_enc, send(mine_enc, TENSOR, 1)],
        [pltpu.VMEM((n_dp * tok, section.shape[1]), BF16)],
        flops=2 * n_dp * tok * section.size,
    )
    kv_grad = kv_grad.reshape(kv_weight.shape)
    swapped = [send(part, TENSOR, 1) for part in parts[:2]]
    far, last, kv_grad = lax.optimization_barrier((*parts[2:], kv_grad))
    parts = [*parts[:2], far, last, *swapped, send(far, TENSOR, 1), send(last, TENSOR, 1)]
    (input_grad,) = call(
        lambda *refs: assemble_kernel(n_dp, n_pipe, n_ten, *refs),
        "input_grad",
        [shaped((tok, width), BF16)],
        [where, *parts],
        [
            pltpu.VMEM((n_dp * n_ten, tok, width // (n_dp * n_ten)), BF16),
            pltpu.SemaphoreType.DMA((n_dp * n_ten,)),
        ],
        space=pl.ANY,
    )
    return (input_grad, kv_grad)


def solution(mesh):
    placed = (
        P(DP, TENSOR),
        P(DP, TENSOR),
        P(DP, None, PIPE, TENSOR),
        P(DP, None, PIPE, TENSOR),
        P(DP, (PIPE, TENSOR)),
        P(DP, (PIPE, TENSOR)),
        P((PIPE, TENSOR), DP),
        P(),
    )
    return jax.shard_map(
        on_device,
        mesh=mesh,
        in_specs=placed,
        out_specs=(P(DP, None), P(DP, None, PIPE, TENSOR)),
        check_vma=False,
    )
```

```python
import math

import jax
import jax.numpy as jnp
from jax import lax
from jax.experimental import pallas as pl
from jax.experimental.pallas import tpu as pltpu
from jax.sharding import PartitionSpec as P

DP, PIPE, TENSOR = "dp", "pipe", "tensor"
BF16, F32 = jnp.bfloat16, jnp.float32


def gelu_parts(preact):
    factor = math.sqrt(2.0 / math.pi)
    tangent = jnp.tanh(factor * (preact + 0.044715 * preact * preact * preact))
    gelu_value = 0.5 * preact * (1.0 + tangent)
    gelu_slope = 0.5 * (1.0 + tangent) + 0.5 * preact * (1.0 - tangent * tangent) * factor * (
        1.0 + 3.0 * 0.044715 * preact * preact
    )
    return (gelu_value, gelu_slope)


def send(value, axis, step):
    if step == 0:
        return value
    size = lax.axis_size(axis)
    return lax.ppermute(value, axis, [(src, src ^ step) for src in range(size)])


def gather(value, axis):
    return [send(value, axis, step) for step in range(lax.axis_size(axis))]


def natural(parts, axis, dim):
    mine = lax.axis_index(axis)
    width = parts[0].shape[dim]
    shape = list(parts[0].shape)
    shape[dim] = width * len(parts)
    out = jnp.zeros(shape, parts[0].dtype)
    for step, part in enumerate(parts):
        out = lax.dynamic_update_slice_in_dim(out, part, (mine ^ step) * width, dim)
    return out


def block(value, axis, step, dim):
    width = value.shape[dim] // lax.axis_size(axis)
    start = (lax.axis_index(axis) ^ step) * width
    return lax.dynamic_slice_in_dim(value, start, width, dim)


def total(blocks, axis):
    out = blocks[0].astype(F32)
    for step in range(1, len(blocks)):
        out = out + send(blocks[step].astype(BF16), axis, step).astype(F32)
    return out


def dot_nt(left, right):
    return lax.dot_general(left, right, (((1,), (1,)), ((), ())), preferred_element_type=F32)


def on_device_any(
    enc_out, mlp_input, grad_kv, kv_weight, gate_weight, up_weight, down_weight, norm_gain
):
    n_dp, n_pipe, n_ten = (lax.axis_size(a) for a in (DP, PIPE, TENSOR))
    tok = grad_kv.shape[0]
    width = norm_gain.shape[0]
    cols = kv_weight.shape[0]
    units = gate_weight.shape[1]
    share = cols // (n_pipe * n_ten)

    grads = jnp.concatenate(gather(grad_kv.reshape(tok, -1), DP), axis=0)

    section = kv_weight.reshape(cols, -1)
    partial = dot_nt(grads, section)
    partial = total([block(partial, TENSOR, k, 1) for k in range(n_ten)], TENSOR)
    partial = total([block(partial, PIPE, k, 1) for k in range(n_pipe)], PIPE)
    partial = partial.astype(BF16).reshape(n_dp, tok, share)
    upstream = jnp.concatenate([send(partial[k], DP, k) for k in range(n_dp)], axis=1)

    down = jnp.concatenate([send(block(down_weight, TENSOR, k, 1), TENSOR, k) for k in range(n_ten)], axis=0)
    down = jnp.concatenate([send(block(down, PIPE, k, 1), PIPE, k) for k in range(n_pipe)], axis=0)
    down = jnp.concatenate(gather(down, DP), axis=1)
    hidden = dot_nt(upstream, down).reshape(tok, n_pipe, n_ten, units)
    hidden = total([hidden[:, :, k] for k in range(n_ten)], TENSOR)
    hidden_grad = total([hidden[:, k] for k in range(n_pipe)], PIPE)

    both = jnp.concatenate([gate_weight, up_weight], axis=1)
    both = jnp.concatenate(gather(both, DP), axis=0)
    resid = natural(gather(mlp_input, TENSOR), TENSOR, 1)
    resid = jnp.concatenate([block(resid, DP, k, 1) for k in range(n_dp)], axis=1)
    gain_row = jnp.concatenate([block(norm_gain, DP, k, 0) for k in range(n_dp)], axis=0).astype(F32)
    values_in = resid.astype(F32)
    row_scale = lax.rsqrt(jnp.mean(values_in * values_in, axis=1, keepdims=True) + 1e-06)
    normed = (values_in * row_scale * gain_row).astype(BF16)
    pre = jnp.dot(normed, both, preferred_element_type=F32)
    gate_pre, up_pre = pre[:, :units], pre[:, units:]

    gelu_value, gelu_slope = gelu_parts(gate_pre)
    gate_grad = hidden_grad * up_pre * gelu_slope
    up_grad = hidden_grad * gelu_value
    dotted = jnp.sum(gate_grad * gate_pre + up_grad * up_pre, axis=1, keepdims=True)
    grads_both = jnp.concatenate([gate_grad, up_grad], axis=1).astype(BF16)
    normed_part = dot_nt(grads_both, both)
    part = row_scale * gain_row * normed_part - values_in * (row_scale * row_scale * (dotted / width))

    part = part.reshape(tok, n_dp, cols)
    part = total([block(part, TENSOR, k, 2) for k in range(n_ten)], TENSOR)
    part = total([block(part, PIPE, k, 2) for k in range(n_pipe)], PIPE)
    part = (part + upstream.reshape(tok, n_dp, share).astype(F32)).astype(BF16)
    whole = natural(gather(part, PIPE), PIPE, 2)
    whole = natural(gather(whole, TENSOR), TENSOR, 2)
    input_grad = natural([whole[:, k] for k in range(n_dp)], DP, 1)

    encoded = natural(gather(enc_out, TENSOR), TENSOR, 1)
    mine = [send(block(block(encoded, DP, k, 1), TENSOR, 0, 1), DP, k) for k in range(n_dp)]
    mine = jnp.concatenate(mine, axis=0)
    mine = natural(gather(mine, TENSOR), TENSOR, 1)
    kv_grad = lax.dot_general(
        mine, grads, (((0,), (0,)), ((), ())), preferred_element_type=F32
    ).astype(BF16)
    return (input_grad, kv_grad.reshape(kv_weight.shape))


def aligned(start, lanes):
    return pl.ds(pl.multiple_of(start, lanes), lanes)


def call(body, name, out, operands, scratch=(), flops=0, space=pltpu.VMEM):
    specs = [pl.BlockSpec(memory_space=pltpu.SMEM)]
    specs += [pl.BlockSpec(memory_space=pltpu.VMEM)] * (len(operands) - 1)
    moved = sum(a.size * a.dtype.itemsize for a in (*operands, *out))
    return pl.pallas_call(
        body,
        name=name,
        out_shape=out,
        in_specs=specs,
        out_specs=[pl.BlockSpec(memory_space=space)] * len(out),
        scratch_shapes=list(scratch),
        compiler_params=pltpu.CompilerParams(vmem_limit_bytes=40 * 1024 * 1024),
        cost_estimate=pl.CostEstimate(flops=flops, bytes_accessed=moved, transcendentals=0),
    )(*operands)


def shaped(shape, dtype):
    return jax.ShapeDtypeStruct(shape, dtype)


def upstream_kernel(n_dp, where, *refs):
    pieces, (section, out, grads) = refs[:n_dp], refs[n_dp:]
    tok = pieces[0].shape[0]
    for k, piece in enumerate(pieces):
        grads[k * tok : (k + 1) * tok, :] = piece[...]
    out[...] = dot_nt(grads[...], section[...]).astype(out.dtype)


def hidden_kernel(n_parts, n_ten, where, mine, other, *refs):
    downs, hidden, outs = refs[:n_parts], refs[n_parts : 2 * n_parts], refs[2 * n_parts : -2]
    upstream, down = refs[-2:]
    upstream[...] = (mine[...].astype(F32) + other[...].astype(F32)).astype(BF16)
    units = downs[0].shape[0]
    for k, part in enumerate(downs):
        down[k * units : (k + 1) * units, :] = part[...]
    result = dot_nt(upstream[...], down[...])
    for k, out in enumerate(hidden):
        out[...] = result[:, k * units : (k + 1) * units].astype(out.dtype)
    for k, out in enumerate(outs):
        tok, half = out.shape
        out[...] = upstream[k * tok : (k + 1) * tok, aligned(where[2] * half, half)]


def last_kernel(where, upstream, down, out):
    out[...] = dot_nt(upstream[...], down[...]).astype(out.dtype)


def owner_kernel(n_dp, n_pipe, where, *refs):
    terms, ups, own, outs = refs[:n_pipe], refs[n_pipe : n_pipe + n_dp - 1], refs[-n_dp], refs[1 - n_dp :]
    tok, units = own.shape
    for k in range(n_dp):
        total_here = terms[0][k * tok : (k + 1) * tok, :]
        for term in terms[1:]:
            total_here = total_here + term[k * tok : (k + 1) * tok, :].astype(F32)
        if k == 0:
            own[...] = total_here
        else:
            outs[k - 1][:, :units] = total_here.astype(BF16)
            outs[k - 1][:, units:] = ups[k - 1][...]


def gate_and_up(packs, k, start, rows):
    pieces = [pack[aligned(start, rows), :] for pack in (packs[k], packs[len(packs) // 2 + k])]
    return jnp.concatenate(pieces, axis=1)


def forward_kernel(n_dp, where, *refs):
    packs, (x_mine, x_other, gain, resid, scale, pre, last, normed) = refs[: 2 * (n_dp - 1)], refs[2 * (n_dp - 1) :]
    ten = where[2]
    half = x_mine.shape[1]
    resid[:, aligned(ten * half, half)] = x_mine[...]
    resid[:, aligned((ten ^ 1) * half, half)] = x_other[...]
    values_in = resid[...].astype(F32)
    row_scale = lax.rsqrt(jnp.mean(values_in * values_in, axis=1, keepdims=True) + 1e-06)
    scale[...] = jnp.broadcast_to(row_scale, scale.shape)
    normed[...] = (values_in * row_scale * gain[...].astype(F32)).astype(BF16)
    cols = resid.shape[1] // n_dp
    result = jnp.zeros(pre.shape, F32)
    for k in range(n_dp - 1):
        left = normed[:, aligned((where[0] ^ k) * cols, cols)]
        result += jnp.dot(left, gate_and_up(packs, k, 0, cols), preferred_element_type=F32)
    last[...] = normed[:, aligned((where[0] ^ (n_dp - 1)) * cols, cols)]
    pre[...] = result


def terms_half(n_dp, n_pipe, n_ten, step, where, grads, pull, packs, scale, resid, gain, out, extra):
    pipe, ten = where[1], where[2]
    cols = resid.shape[1] // n_dp
    half = cols // n_ten
    share = half // n_pipe
    start = (ten ^ step) * half
    for k in range(n_dp):
        i = where[0] ^ k
        spot = aligned(i * cols + start, half)
        part = dot_nt(grads, gate_and_up(packs, k, start, half))
        part = scale * (gain[:, spot].astype(F32) * part) - resid[:, spot].astype(F32) * pull
        if extra is not None:
            part = part + extra[k][...].astype(F32)
        part = part.astype(out.dtype)
        for j in range(n_pipe):
            out[pipe ^ j, :, aligned(i * share, share)] = part[:, j * share : (j + 1) * share]


def backward_kernel(n_dp, n_pipe, n_ten, where, *refs):
    terms, packs = refs[:n_dp], refs[n_dp : 3 * n_dp]
    pre, last, scale, resid, gain, other, grads, pull = refs[3 * n_dp :]
    units = terms[0].shape[1]
    hidden_grad = terms[0][...]
    for term in terms[1:]:
        hidden_grad = hidden_grad + term[:, :units].astype(F32)
    both = gate_and_up(packs, n_dp - 1, 0, last.shape[1])
    pre_here = pre[...] + jnp.dot(last[...], both, preferred_element_type=F32)
    gate_pre, up_pre = pre_here[:, :units], pre_here[:, units:]
    gelu_value, gelu_slope = gelu_parts(gate_pre)
    gate_grad = hidden_grad * up_pre * gelu_slope
    up_grad = hidden_grad * gelu_value
    dotted = jnp.sum(gate_grad * gate_pre + up_grad * up_pre, axis=1, keepdims=True)
    grads[...] = jnp.concatenate([gate_grad, up_grad], axis=1).astype(BF16)
    row_scale = scale[:, :1]
    pull_here = row_scale * row_scale * (dotted / resid.shape[1])
    pull[...] = jnp.broadcast_to(pull_here, pull.shape)
    terms_half(
        n_dp, n_pipe, n_ten, 1, where, grads[...], pull_here, packs, row_scale, resid, gain, other, None
    )


def own_kernel(n_dp, n_pipe, n_ten, where, grads, pull, *refs):
    terms, upstream, packs = refs[: n_dp - 1], refs[n_dp - 1], refs[n_dp : 3 * n_dp]
    scale, resid, gain, mine = refs[3 * n_dp :]
    half = upstream.shape[1]
    extra = [upstream] + [term.at[:, term.shape[1] - half :] for term in terms]
    terms_half(
        n_dp, n_pipe, n_ten, 0, where, grads[...], pull[:, :1], packs, scale[:, :1], resid, gain, mine, extra
    )


def assemble_kernel(n_dp, n_pipe, n_ten, where, *refs):
    parts, (out, held, sems) = refs[:-3], refs[-3:]
    pipe, ten = where[1], where[2]
    share = parts[0].shape[1] // n_dp
    width = share * n_pipe
    copies = []
    for i in range(n_dp):
        for core in range(n_ten):
            at = i * n_ten + core
            for k in range(n_pipe):
                part = parts[core * n_pipe + k]
                held[at, :, aligned((pipe ^ k) * share, share)] = part[:, i * share : (i + 1) * share]
            spot = aligned((i * n_ten + (ten ^ core)) * width, width)
            copies.append(pltpu.make_async_copy(held.at[at], out.at[:, spot], sems.at[at]))
            copies[-1].start()
    for copy in copies:
        copy.wait()


def encoded_kernel(n_dp, n_ten, where, mine, other, own, near, far):
    dp, ten = where[0], where[2]
    tok, half = own.shape
    held = n_dp // n_ten
    for k, out in ((0, own), (1, near.at[:tok]), (3, near.at[tok:]), (2, far)):
        i = dp ^ k
        spot = aligned((lax.rem(i, held) * n_ten + ten) * half, half)
        here = i // held == ten

        @pl.when(here)
        def _(out=out, spot=spot):
            out[...] = mine[:, spot]

        @pl.when(jnp.logical_not(here))
        def _(out=out, spot=spot):
            out[...] = other[:, spot]


def kv_kernel(n_dp, where, *refs):
    pieces, (enc_mine, enc_other, out, grads) = refs[:n_dp], refs[n_dp:]
    tok = pieces[0].shape[0]
    half = enc_mine.shape[1]
    for k, piece in enumerate(pieces):
        grads[k * tok : (k + 1) * tok, :] = piece[...]
    for step, enc in ((0, enc_mine), (1, enc_other)):
        out[aligned((where[2] ^ step) * half, half), :] = lax.dot_general(
            enc[...], grads[...], (((0,), (0,)), ((), ())), preferred_element_type=F32
        ).astype(out.dtype)


def on_device(
    enc_out, mlp_input, grad_kv, kv_weight, gate_weight, up_weight, down_weight, norm_gain
):
    n_dp, n_pipe, n_ten = (lax.axis_size(a) for a in (DP, PIPE, TENSOR))
    tok = grad_kv.shape[0]
    width = norm_gain.shape[0]
    cols = kv_weight.shape[0]
    units = gate_weight.shape[1]
    share = cols // (n_pipe * n_ten)
    squares = n_dp == n_pipe == n_ten * n_ten and n_ten == 2
    if not squares or share % 128 or tok % 128 or units % 128:
        return on_device_any(
            enc_out, mlp_input, grad_kv, kv_weight, gate_weight, up_weight, down_weight, norm_gain
        )
    where = jnp.stack([lax.axis_index(a) for a in (DP, PIPE, TENSOR)]).astype(jnp.int32)

    grads = gather(grad_kv.reshape(tok, -1), DP)
    x_other = send(mlp_input, TENSOR, 1)
    far, near = send(down_weight, PIPE, 2), send(down_weight, PIPE, 1)
    grads, gate, up = lax.optimization_barrier((grads, gate_weight, up_weight))
    gates = [gate, send(gate, DP, 1), send(gate, DP, 2)]
    ups = [up, send(up, DP, 1), send(up, DP, 2)]
    grads, far, near = lax.optimization_barrier((grads, far, near))
    downs = [down_weight, near, far, send(far, PIPE, 1)]

    section = kv_weight.reshape(cols, -1)
    half = cols // n_ten
    (mine,) = call(
        lambda *refs: upstream_kernel(n_dp, *refs),
        "upstream_terms",
        [shaped((n_dp * tok, cols), BF16)],
        [where, *grads, section],
        [pltpu.VMEM((n_dp * tok, section.shape[1]), BF16)],
        flops=2 * n_dp * tok * section.size,
    )
    other = send(mine, TENSOR, 1)
    enc_other = send(enc_out, TENSOR, 1)
    other, x_other, enc_other = lax.optimization_barrier((other, x_other, enc_other))
    group = n_pipe * units
    outs = call(
        lambda *refs: hidden_kernel(n_pipe - 1, n_ten, *refs),
        "hidden_terms",
        [shaped((n_dp * tok, units), F32)]
        + [shaped((n_dp * tok, units), BF16)] * (n_pipe - 2)
        + [shaped((tok, half), BF16)] * n_dp
        + [shaped((n_dp * tok, cols), BF16)],
        [where, mine, other, *downs[:-1]],
        [pltpu.VMEM((group - units, cols), BF16)],
        flops=2 * n_dp * tok * cols * group,
    )
    *outs, upstream = outs
    (last_out,) = call(
        last_kernel,
        "hidden_last",
        [shaped((n_dp * tok, units), BF16)],
        [where, upstream, downs[-1]],
        flops=2 * n_dp * tok * cols * units,
    )
    outs = [*outs[: n_pipe - 1], last_out, *outs[n_pipe - 1 :]]
    terms = [send(out, PIPE, k) for k, out in enumerate(outs[:n_pipe])]
    gain_row = norm_gain.reshape(1, width)
    resid, scale, pre, last = call(
        lambda *refs: forward_kernel(n_dp, *refs),
        "mlp_forward",
        [shaped((tok, width), BF16), shaped((tok, 128), F32), shaped((tok, 2 * units), F32), shaped((tok, cols), BF16)],
        [where, *gates, *ups, mlp_input, x_other, gain_row],
        [pltpu.VMEM((tok, width), BF16)],
        flops=4 * tok * width * units,
    )
    packs = [*gates, send(gates[1], DP, 2), *ups, send(ups[2], DP, 1)]
    terms, resid, scale, pre, last = lax.optimization_barrier((terms, resid, scale, pre, last))
    hidden, *sums = call(
        lambda *refs: owner_kernel(n_dp, n_pipe, *refs),
        "hidden_sums",
        [shaped((tok, units), F32)] + [shaped((tok, units + half), BF16)] * (n_dp - 1),
        [where, *terms, *outs[n_pipe + 1 :]],
    )
    terms = [hidden] + [send(part, DP, k) for k, part in enumerate(sums, 1)]
    encoded = [enc_out, enc_other]
    encoded = call(
        lambda *refs: encoded_kernel(n_dp, n_ten, *refs),
        "encoded_blocks",
        [shaped((tok, half), BF16), shaped((2 * tok, half), BF16), shaped((tok, half), BF16)],
        [where, *encoded],
    )
    terms, encoded = lax.optimization_barrier((terms, encoded))

    other, grads_both, pull = call(
        lambda *refs: backward_kernel(n_dp, n_pipe, n_ten, *refs),
        "mlp_backward",
        [shaped((n_pipe, tok, n_dp * share), BF16), shaped((tok, 2 * units), BF16), shaped((tok, 128), F32)],
        [where, *terms, *packs, pre, last, scale, resid, gain_row],
        flops=2 * tok * width * units,
    )
    (mine,) = call(
        lambda *refs: own_kernel(n_dp, n_pipe, n_ten, *refs),
        "own_terms",
        [shaped((n_pipe, tok, n_dp * share), F32)],
        [where, grads_both, pull, *terms[1:], outs[n_pipe], *packs, scale, resid, gain_row],
        flops=2 * tok * width * units,
    )
    mine = mine + send(other, TENSOR, 1).astype(F32)
    first = send(encoded[1], DP, 1)
    second = jnp.concatenate([encoded[2], first[tok:]], axis=0)
    mine, second = lax.optimization_barrier((mine, second))
    terms = [send(mine[k].astype(BF16), PIPE, k) for k in range(1, n_pipe)]
    second = send(second, DP, 2)
    part = mine[0]
    for term in terms:
        part = part + term.astype(F32)
    part = part.astype(BF16)
    part, second = lax.optimization_barrier((part, second))
    parts = gather(part, PIPE)

    mine_enc = jnp.concatenate([encoded[0], first[:tok], second], axis=0)
    (kv_grad,) = call(
        lambda *refs: kv_kernel(n_dp, *refs),
        "kv_grad",
        [shaped((cols, section.shape[1]), BF16)],
        [where, *grads, mine_enc, send(mine_enc, TENSOR, 1)],
        [pltpu.VMEM((n_dp * tok, section.shape[1]), BF16)],
        flops=2 * n_dp * tok * section.size,
    )
    kv_grad = kv_grad.reshape(kv_weight.shape)
    swapped = [send(part, TENSOR, 1) for part in parts[:2]]
    far, last, kv_grad = lax.optimization_barrier((*parts[2:], kv_grad))
    parts = [*parts[:2], far, last, *swapped, send(far, TENSOR, 1), send(last, TENSOR, 1)]
    (input_grad,) = call(
        lambda *refs: assemble_kernel(n_dp, n_pipe, n_ten, *refs),
        "input_grad",
        [shaped((tok, width), BF16)],
        [where, *parts],
        [
            pltpu.VMEM((n_dp * n_ten, tok, width // (n_dp * n_ten)), BF16),
            pltpu.SemaphoreType.DMA((n_dp * n_ten,)),
        ],
        space=pl.ANY,
    )
    return (input_grad, kv_grad)


def solution(mesh):
    placed = (
        P(DP, TENSOR),
        P(DP, TENSOR),
        P(DP, None, PIPE, TENSOR),
        P(DP, None, PIPE, TENSOR),
        P(DP, (PIPE, TENSOR)),
        P(DP, (PIPE, TENSOR)),
        P((PIPE, TENSOR), DP),
        P(),
    )
    return jax.shard_map(
        on_device,
        mesh=mesh,
        in_specs=placed,
        out_specs=(P(DP, None), P(DP, None, PIPE, TENSOR)),
        check_vma=False,
    )
```

```python
import math

import jax
import jax.numpy as jnp
from jax import lax
from jax.experimental import pallas as pl
from jax.experimental.pallas import tpu as pltpu
from jax.sharding import PartitionSpec as P

DP, PIPE, TENSOR = "dp", "pipe", "tensor"
BF16, F32 = jnp.bfloat16, jnp.float32


def gelu_parts(preact):
    factor = math.sqrt(2.0 / math.pi)
    tangent = jnp.tanh(factor * (preact + 0.044715 * preact * preact * preact))
    gelu_value = 0.5 * preact * (1.0 + tangent)
    gelu_slope = 0.5 * (1.0 + tangent) + 0.5 * preact * (1.0 - tangent * tangent) * factor * (
        1.0 + 3.0 * 0.044715 * preact * preact
    )
    return (gelu_value, gelu_slope)


def send(value, axis, step):
    if step == 0:
        return value
    size = lax.axis_size(axis)
    return lax.ppermute(value, axis, [(src, src ^ step) for src in range(size)])


def gather(value, axis):
    return [send(value, axis, step) for step in range(lax.axis_size(axis))]


def natural(parts, axis, dim):
    mine = lax.axis_index(axis)
    width = parts[0].shape[dim]
    shape = list(parts[0].shape)
    shape[dim] = width * len(parts)
    out = jnp.zeros(shape, parts[0].dtype)
    for step, part in enumerate(parts):
        out = lax.dynamic_update_slice_in_dim(out, part, (mine ^ step) * width, dim)
    return out


def block(value, axis, step, dim):
    width = value.shape[dim] // lax.axis_size(axis)
    start = (lax.axis_index(axis) ^ step) * width
    return lax.dynamic_slice_in_dim(value, start, width, dim)


def total(blocks, axis):
    out = blocks[0].astype(F32)
    for step in range(1, len(blocks)):
        out = out + send(blocks[step].astype(BF16), axis, step).astype(F32)
    return out


def dot_nt(left, right):
    return lax.dot_general(left, right, (((1,), (1,)), ((), ())), preferred_element_type=F32)


def on_device_any(
    enc_out, mlp_input, grad_kv, kv_weight, gate_weight, up_weight, down_weight, norm_gain
):
    n_dp, n_pipe, n_ten = (lax.axis_size(a) for a in (DP, PIPE, TENSOR))
    tok = grad_kv.shape[0]
    width = norm_gain.shape[0]
    cols = kv_weight.shape[0]
    units = gate_weight.shape[1]
    share = cols // (n_pipe * n_ten)

    grads = jnp.concatenate(gather(grad_kv.reshape(tok, -1), DP), axis=0)

    section = kv_weight.reshape(cols, -1)
    partial = dot_nt(grads, section)
    partial = total([block(partial, TENSOR, k, 1) for k in range(n_ten)], TENSOR)
    partial = total([block(partial, PIPE, k, 1) for k in range(n_pipe)], PIPE)
    partial = partial.astype(BF16).reshape(n_dp, tok, share)
    upstream = jnp.concatenate([send(partial[k], DP, k) for k in range(n_dp)], axis=1)

    down = jnp.concatenate([send(block(down_weight, TENSOR, k, 1), TENSOR, k) for k in range(n_ten)], axis=0)
    down = jnp.concatenate([send(block(down, PIPE, k, 1), PIPE, k) for k in range(n_pipe)], axis=0)
    down = jnp.concatenate(gather(down, DP), axis=1)
    hidden = dot_nt(upstream, down).reshape(tok, n_pipe, n_ten, units)
    hidden = total([hidden[:, :, k] for k in range(n_ten)], TENSOR)
    hidden_grad = total([hidden[:, k] for k in range(n_pipe)], PIPE)

    both = jnp.concatenate([gate_weight, up_weight], axis=1)
    both = jnp.concatenate(gather(both, DP), axis=0)
    resid = natural(gather(mlp_input, TENSOR), TENSOR, 1)
    resid = jnp.concatenate([block(resid, DP, k, 1) for k in range(n_dp)], axis=1)
    gain_row = jnp.concatenate([block(norm_gain, DP, k, 0) for k in range(n_dp)], axis=0).astype(F32)
    values_in = resid.astype(F32)
    row_scale = lax.rsqrt(jnp.mean(values_in * values_in, axis=1, keepdims=True) + 1e-06)
    normed = (values_in * row_scale * gain_row).astype(BF16)
    pre = jnp.dot(normed, both, preferred_element_type=F32)
    gate_pre, up_pre = pre[:, :units], pre[:, units:]

    gelu_value, gelu_slope = gelu_parts(gate_pre)
    gate_grad = hidden_grad * up_pre * gelu_slope
    up_grad = hidden_grad * gelu_value
    dotted = jnp.sum(gate_grad * gate_pre + up_grad * up_pre, axis=1, keepdims=True)
    grads_both = jnp.concatenate([gate_grad, up_grad], axis=1).astype(BF16)
    normed_part = dot_nt(grads_both, both)
    part = row_scale * gain_row * normed_part - values_in * (row_scale * row_scale * (dotted / width))

    part = part.reshape(tok, n_dp, cols)
    part = total([block(part, TENSOR, k, 2) for k in range(n_ten)], TENSOR)
    part = total([block(part, PIPE, k, 2) for k in range(n_pipe)], PIPE)
    part = (part + upstream.reshape(tok, n_dp, share).astype(F32)).astype(BF16)
    whole = natural(gather(part, PIPE), PIPE, 2)
    whole = natural(gather(whole, TENSOR), TENSOR, 2)
    input_grad = natural([whole[:, k] for k in range(n_dp)], DP, 1)

    encoded = natural(gather(enc_out, TENSOR), TENSOR, 1)
    mine = [send(block(block(encoded, DP, k, 1), TENSOR, 0, 1), DP, k) for k in range(n_dp)]
    mine = jnp.concatenate(mine, axis=0)
    mine = natural(gather(mine, TENSOR), TENSOR, 1)
    kv_grad = lax.dot_general(
        mine, grads, (((0,), (0,)), ((), ())), preferred_element_type=F32
    ).astype(BF16)
    return (input_grad, kv_grad.reshape(kv_weight.shape))


def aligned(start, lanes):
    return pl.ds(pl.multiple_of(start, lanes), lanes)


def call(body, name, out, operands, scratch=(), flops=0, space=pltpu.VMEM):
    specs = [pl.BlockSpec(memory_space=pltpu.SMEM)]
    specs += [pl.BlockSpec(memory_space=pltpu.VMEM)] * (len(operands) - 1)
    moved = sum(a.size * a.dtype.itemsize for a in (*operands, *out))
    return pl.pallas_call(
        body,
        name=name,
        out_shape=out,
        in_specs=specs,
        out_specs=[pl.BlockSpec(memory_space=space)] * len(out),
        scratch_shapes=list(scratch),
        compiler_params=pltpu.CompilerParams(vmem_limit_bytes=40 * 1024 * 1024),
        cost_estimate=pl.CostEstimate(flops=flops, bytes_accessed=moved, transcendentals=0),
    )(*operands)


def shaped(shape, dtype):
    return jax.ShapeDtypeStruct(shape, dtype)


def upstream_kernel(n_dp, where, *refs):
    pieces, (section, out, grads) = refs[:n_dp], refs[n_dp:]
    tok = pieces[0].shape[0]
    for k, piece in enumerate(pieces):
        grads[k * tok : (k + 1) * tok, :] = piece[...]
    out[...] = dot_nt(grads[...], section[...]).astype(out.dtype)


def hidden_kernel(n_parts, n_ten, where, mine, other, *refs):
    downs, hidden, outs = refs[:n_parts], refs[n_parts : 2 * n_parts], refs[2 * n_parts : -2]
    upstream, down = refs[-2:]
    upstream[...] = (mine[...].astype(F32) + other[...].astype(F32)).astype(BF16)
    units = downs[0].shape[0]
    for k, part in enumerate(downs):
        down[k * units : (k + 1) * units, :] = part[...]
    result = dot_nt(upstream[...], down[...])
    for k, out in enumerate(hidden):
        out[...] = result[:, k * units : (k + 1) * units].astype(out.dtype)
    for k, out in enumerate(outs):
        tok, half = out.shape
        out[...] = upstream[k * tok : (k + 1) * tok, aligned(where[2] * half, half)]


def owner_kernel(n_dp, n_pipe, where, *refs):
    terms, ups, own, outs = refs[:n_pipe], refs[n_pipe : n_pipe + n_dp - 1], refs[-n_dp], refs[1 - n_dp :]
    tok, units = own.shape
    for k in range(n_dp):
        total_here = terms[0][k * tok : (k + 1) * tok, :]
        for term in terms[1:]:
            total_here = total_here + term[k * tok : (k + 1) * tok, :].astype(F32)
        if k == 0:
            own[...] = total_here
        else:
            outs[k - 1][:, :units] = total_here.astype(BF16)
            outs[k - 1][:, units:] = ups[k - 1][...]


def gate_and_up(packs, k, start, rows):
    pieces = [pack[aligned(start, rows), :] for pack in (packs[k], packs[len(packs) // 2 + k])]
    return jnp.concatenate(pieces, axis=1)


def forward_kernel(n_dp, where, *refs):
    packs, (x_mine, x_other, gain, resid, scale, pre, last, normed) = refs[: 2 * (n_dp - 1)], refs[2 * (n_dp - 1) :]
    ten = where[2]
    half = x_mine.shape[1]
    resid[:, aligned(ten * half, half)] = x_mine[...]
    resid[:, aligned((ten ^ 1) * half, half)] = x_other[...]
    values_in = resid[...].astype(F32)
    row_scale = lax.rsqrt(jnp.mean(values_in * values_in, axis=1, keepdims=True) + 1e-06)
    scale[...] = jnp.broadcast_to(row_scale, scale.shape)
    normed[...] = (values_in * row_scale * gain[...].astype(F32)).astype(BF16)
    cols = resid.shape[1] // n_dp
    result = jnp.zeros(pre.shape, F32)
    for k in range(n_dp - 1):
        left = normed[:, aligned((where[0] ^ k) * cols, cols)]
        result += jnp.dot(left, gate_and_up(packs, k, 0, cols), preferred_element_type=F32)
    last[...] = normed[:, aligned((where[0] ^ (n_dp - 1)) * cols, cols)]
    pre[...] = result


def terms_half(n_dp, n_pipe, n_ten, step, where, grads, pull, packs, scale, resid, gain, out, extra):
    pipe, ten = where[1], where[2]
    cols = resid.shape[1] // n_dp
    half = cols // n_ten
    share = half // n_pipe
    start = (ten ^ step) * half
    for k in range(n_dp):
        i = where[0] ^ k
        spot = aligned(i * cols + start, half)
        part = dot_nt(grads, gate_and_up(packs, k, start, half))
        part = scale * (gain[:, spot].astype(F32) * part) - resid[:, spot].astype(F32) * pull
        if extra is not None:
            part = part + extra[k][...].astype(F32)
        part = part.astype(out.dtype)
        for j in range(n_pipe):
            out[pipe ^ j, :, aligned(i * share, share)] = part[:, j * share : (j + 1) * share]


def backward_kernel(n_dp, n_pipe, n_ten, where, *refs):
    terms, packs = refs[:n_dp], refs[n_dp : 3 * n_dp]
    pre, last, scale, resid, gain, other, grads, pull = refs[3 * n_dp :]
    units = terms[0].shape[1]
    hidden_grad = terms[0][...]
    for term in terms[1:]:
        hidden_grad = hidden_grad + term[:, :units].astype(F32)
    both = gate_and_up(packs, n_dp - 1, 0, last.shape[1])
    pre_here = pre[...] + jnp.dot(last[...], both, preferred_element_type=F32)
    gate_pre, up_pre = pre_here[:, :units], pre_here[:, units:]
    gelu_value, gelu_slope = gelu_parts(gate_pre)
    gate_grad = hidden_grad * up_pre * gelu_slope
    up_grad = hidden_grad * gelu_value
    dotted = jnp.sum(gate_grad * gate_pre + up_grad * up_pre, axis=1, keepdims=True)
    grads[...] = jnp.concatenate([gate_grad, up_grad], axis=1).astype(BF16)
    row_scale = scale[:, :1]
    pull_here = row_scale * row_scale * (dotted / resid.shape[1])
    pull[...] = jnp.broadcast_to(pull_here, pull.shape)
    terms_half(
        n_dp, n_pipe, n_ten, 1, where, grads[...], pull_here, packs, row_scale, resid, gain, other, None
    )


def own_kernel(n_dp, n_pipe, n_ten, where, grads, pull, *refs):
    terms, upstream, packs = refs[: n_dp - 1], refs[n_dp - 1], refs[n_dp : 3 * n_dp]
    scale, resid, gain, mine = refs[3 * n_dp :]
    half = upstream.shape[1]
    extra = [upstream] + [term.at[:, term.shape[1] - half :] for term in terms]
    terms_half(
        n_dp, n_pipe, n_ten, 0, where, grads[...], pull[:, :1], packs, scale[:, :1], resid, gain, mine, extra
    )


def assemble_kernel(n_dp, n_pipe, n_ten, where, *refs):
    parts, (out, held, sems) = refs[:-3], refs[-3:]
    pipe, ten = where[1], where[2]
    share = parts[0].shape[1] // n_dp
    width = share * n_pipe
    copies = []
    for i in range(n_dp):
        for core in range(n_ten):
            at = i * n_ten + core
            for k in range(n_pipe):
                part = parts[core * n_pipe + k]
                held[at, :, aligned((pipe ^ k) * share, share)] = part[:, i * share : (i + 1) * share]
            spot = aligned((i * n_ten + (ten ^ core)) * width, width)
            copies.append(pltpu.make_async_copy(held.at[at], out.at[:, spot], sems.at[at]))
            copies[-1].start()
    for copy in copies:
        copy.wait()


def encoded_kernel(n_dp, n_ten, where, mine, other, own, near, far):
    dp, ten = where[0], where[2]
    tok, half = own.shape
    held = n_dp // n_ten
    for k, out in ((0, own), (1, near.at[:tok]), (3, near.at[tok:]), (2, far)):
        i = dp ^ k
        spot = aligned((lax.rem(i, held) * n_ten + ten) * half, half)
        here = i // held == ten

        @pl.when(here)
        def _(out=out, spot=spot):
            out[...] = mine[:, spot]

        @pl.when(jnp.logical_not(here))
        def _(out=out, spot=spot):
            out[...] = other[:, spot]


def kv_kernel(n_dp, where, *refs):
    pieces, (enc_mine, enc_other, out, grads) = refs[:n_dp], refs[n_dp:]
    tok = pieces[0].shape[0]
    half = enc_mine.shape[1]
    for k, piece in enumerate(pieces):
        grads[k * tok : (k + 1) * tok, :] = piece[...]
    for step, enc in ((0, enc_mine), (1, enc_other)):
        out[aligned((where[2] ^ step) * half, half), :] = lax.dot_general(
            enc[...], grads[...], (((0,), (0,)), ((), ())), preferred_element_type=F32
        ).astype(out.dtype)


def on_device(
    enc_out, mlp_input, grad_kv, kv_weight, gate_weight, up_weight, down_weight, norm_gain
):
    n_dp, n_pipe, n_ten = (lax.axis_size(a) for a in (DP, PIPE, TENSOR))
    tok = grad_kv.shape[0]
    width = norm_gain.shape[0]
    cols = kv_weight.shape[0]
    units = gate_weight.shape[1]
    share = cols // (n_pipe * n_ten)
    squares = n_dp == n_pipe == n_ten * n_ten and n_ten == 2
    if not squares or share % 128 or tok % 128 or units % 128:
        return on_device_any(
            enc_out, mlp_input, grad_kv, kv_weight, gate_weight, up_weight, down_weight, norm_gain
        )
    where = jnp.stack([lax.axis_index(a) for a in (DP, PIPE, TENSOR)]).astype(jnp.int32)

    grads = gather(grad_kv.reshape(tok, -1), DP)
    x_other = send(mlp_input, TENSOR, 1)
    far, near = send(down_weight, PIPE, 2), send(down_weight, PIPE, 1)
    grads, gate, up = lax.optimization_barrier((grads, gate_weight, up_weight))
    far, first_gate, first_up = lax.optimization_barrier((far, gate_weight, up_weight))
    gates = [gate, send(first_gate, DP, 1), send(gate, DP, 2)]
    ups = [up, send(up, DP, 1), send(first_up, DP, 2)]
    grads, far, near = lax.optimization_barrier((grads, far, near))
    downs = [down_weight, near, far, send(far, PIPE, 1)]

    section = kv_weight.reshape(cols, -1)
    half = cols // n_ten
    (mine,) = call(
        lambda *refs: upstream_kernel(n_dp, *refs),
        "upstream_terms",
        [shaped((n_dp * tok, cols), BF16)],
        [where, *grads, section],
        [pltpu.VMEM((n_dp * tok, section.shape[1]), BF16)],
        flops=2 * n_dp * tok * section.size,
    )
    other = send(mine, TENSOR, 1)
    enc_other = send(enc_out, TENSOR, 1)
    other, x_other, enc_other = lax.optimization_barrier((other, x_other, enc_other))
    group = n_pipe * units
    outs = call(
        lambda *refs: hidden_kernel(n_pipe - 1, n_ten, *refs),
        "hidden_terms",
        [shaped((n_dp * tok, units), F32)]
        + [shaped((n_dp * tok, units), BF16)] * (n_pipe - 2)
        + [shaped((tok, half), BF16)] * n_dp,
        [where, mine, other, *downs[:-1]],
        [pltpu.VMEM((n_dp * tok, cols), BF16), pltpu.VMEM((group - units, cols), BF16)],
        flops=2 * n_dp * tok * cols * group,
    )
    (last_out,) = call(
        lambda *refs: hidden_kernel(1, n_ten, *refs),
        "hidden_last",
        [shaped((n_dp * tok, units), BF16)],
        [where, mine, other, downs[-1]],
        [pltpu.VMEM((n_dp * tok, cols), BF16), pltpu.VMEM((units, cols), BF16)],
        flops=2 * n_dp * tok * cols * units,
    )
    outs = [*outs[: n_pipe - 1], last_out, *outs[n_pipe - 1 :]]
    terms = [send(out, PIPE, k) for k, out in enumerate(outs[:n_pipe])]
    gain_row = norm_gain.reshape(1, width)
    resid, scale, pre, last = call(
        lambda *refs: forward_kernel(n_dp, *refs),
        "mlp_forward",
        [shaped((tok, width), BF16), shaped((tok, 128), F32), shaped((tok, 2 * units), F32), shaped((tok, cols), BF16)],
        [where, *gates, *ups, mlp_input, x_other, gain_row],
        [pltpu.VMEM((tok, width), BF16)],
        flops=4 * tok * width * units,
    )
    packs = [*gates, send(gates[1], DP, 2), *ups, send(ups[2], DP, 1)]
    terms, resid, scale, pre, last = lax.optimization_barrier((terms, resid, scale, pre, last))
    hidden, *sums = call(
        lambda *refs: owner_kernel(n_dp, n_pipe, *refs),
        "hidden_sums",
        [shaped((tok, units), F32)] + [shaped((tok, units + half), BF16)] * (n_dp - 1),
        [where, *terms, *outs[n_pipe + 1 :]],
    )
    terms = [hidden] + [send(part, DP, k) for k, part in enumerate(sums, 1)]
    encoded = [enc_out, enc_other]
    encoded = call(
        lambda *refs: encoded_kernel(n_dp, n_ten, *refs),
        "encoded_blocks",
        [shaped((tok, half), BF16), shaped((2 * tok, half), BF16), shaped((tok, half), BF16)],
        [where, *encoded],
    )
    terms, encoded = lax.optimization_barrier((terms, encoded))

    other, grads_both, pull = call(
        lambda *refs: backward_kernel(n_dp, n_pipe, n_ten, *refs),
        "mlp_backward",
        [shaped((n_pipe, tok, n_dp * share), BF16), shaped((tok, 2 * units), BF16), shaped((tok, 128), F32)],
        [where, *terms, *packs, pre, last, scale, resid, gain_row],
        flops=2 * tok * width * units,
    )
    (mine,) = call(
        lambda *refs: own_kernel(n_dp, n_pipe, n_ten, *refs),
        "own_terms",
        [shaped((n_pipe, tok, n_dp * share), F32)],
        [where, grads_both, pull, *terms[1:], outs[n_pipe], *packs, scale, resid, gain_row],
        flops=2 * tok * width * units,
    )
    mine = mine + send(other, TENSOR, 1).astype(F32)
    first = send(encoded[1], DP, 1)
    second = jnp.concatenate([encoded[2], first[tok:]], axis=0)
    mine, second = lax.optimization_barrier((mine, second))
    terms = [send(mine[k].astype(BF16), PIPE, k) for k in range(1, n_pipe)]
    second = send(second, DP, 2)
    part = mine[0]
    for term in terms:
        part = part + term.astype(F32)
    part = part.astype(BF16)
    part, second = lax.optimization_barrier((part, second))
    parts = gather(part, PIPE)

    mine_enc = jnp.concatenate([encoded[0], first[:tok], second], axis=0)
    (kv_grad,) = call(
        lambda *refs: kv_kernel(n_dp, *refs),
        "kv_grad",
        [shaped((cols, section.shape[1]), BF16)],
        [where, *grads, mine_enc, send(mine_enc, TENSOR, 1)],
        [pltpu.VMEM((n_dp * tok, section.shape[1]), BF16)],
        flops=2 * n_dp * tok * section.size,
    )
    kv_grad = kv_grad.reshape(kv_weight.shape)
    swapped = [send(part, TENSOR, 1) for part in parts[:2]]
    far, last, kv_grad = lax.optimization_barrier((*parts[2:], kv_grad))
    parts = [*parts[:2], far, last, *swapped, send(far, TENSOR, 1), send(last, TENSOR, 1)]
    (input_grad,) = call(
        lambda *refs: assemble_kernel(n_dp, n_pipe, n_ten, *refs),
        "input_grad",
        [shaped((tok, width), BF16)],
        [where, *parts],
        [
            pltpu.VMEM((n_dp * n_ten, tok, width // (n_dp * n_ten)), BF16),
            pltpu.SemaphoreType.DMA((n_dp * n_ten,)),
        ],
        space=pl.ANY,
    )
    return (input_grad, kv_grad)


def solution(mesh):
    placed = (
        P(DP, TENSOR),
        P(DP, TENSOR),
        P(DP, None, PIPE, TENSOR),
        P(DP, None, PIPE, TENSOR),
        P(DP, (PIPE, TENSOR)),
        P(DP, (PIPE, TENSOR)),
        P((PIPE, TENSOR), DP),
        P(),
    )
    return jax.shard_map(
        on_device,
        mesh=mesh,
        in_specs=placed,
        out_specs=(P(DP, None), P(DP, None, PIPE, TENSOR)),
        check_vma=False,
    )
```
